32 devices in a mesh: group: 2 (over y), tok: 4 (over z), head: 2 (over x), sub: 2 (over core).
Axes of the slice: x: 2, y: 2, z: 4, core: 2. Of those that a mesh axis runs over, the one named last changes fastest.
Arguments:
- hidden_in: bfloat16 [4096, 4096], P(('group', 'tok')), parts along dimension 0, may hold values from -6 to 6
- norm_gain: bfloat16 [4096], replicated, may hold values from 0.099609375 to 1.8984375
- q_weight: bfloat16 [4096, 1024], P('tok', ('head', 'sub'))
- kv_weight: bfloat16 [4096, 512], P('tok', ('head', 'sub')), may hold values from -0.09375 to 0.09375
- o_weight: bfloat16 [1024, 4096], P(('head', 'sub'), 'tok'), may hold values from -0.25 to 0.25
- doc_lengths: int32 [8], P('group'), parts along dimension 0, may hold values from 1 to 1024, 2048 in all
- task_server: int32 [32, 8], P('group'), parts along dimension 0, may hold values from 0 to 7, as said below
Outputs:
- layer_out: bfloat16 [4096, 4096], P(('group', 'tok'), ('head', 'sub')), parts along dimension 0
- task_lse: float32 [16, 8, 2, 128], P(('group', 'tok', 'sub'), None, 'head'), parts along dimension 0
The draws below stay inside these ranges and needn't reach their ends.
There are 2 independent parts, one for each index of `group`. The reference program is written for one: setup_inputs(seed, part) draws one part's arguments, and reference() takes and returns one part's arrays. A program takes and returns all parts, laid end to end along the dimension named above; an argument that names none is the same for every part. Nothing has to cross between parts.
Inputs may be any that keep to these rules, and one draw needn't show every extreme that they name: `doc_lengths`: documents are laid end to end from token 0; the lengths sum to 2048 and the longest is 1024. `task_server`: A server is a token device's index among 8. Within each KV head, the 8 tasks of one token device j (its query blocks for its 2 query heads, j as in the reference program) name distinct servers, and one server is named by one task of every token device.
All inputs are finite; a program needn't handle non-finite values.
Results may differ from the reference program's by a relative error of at most 0.0095.
The reference program's roundings to bfloat16 on the way count: a program that leaves them out, or rounds other values in their place, can miss the bound.
Values may be sent and summed in bfloat16 or wider, within the bound.
A program may use at most 64 MiB of HBM per device.

```python
import math
import jax
import jax.numpy as jnp
import numpy as np
from jax import lax

D = 4096
GQ = 4
HD = 128
BLOCK = 128
TOK_DEV = 512
KVH = 2
QH = 8
HEADS_DEV = 2
TOKENS = 2048
BLK_DEV = 4
TASKS = 8
SERVERS = 8
NBLK = 16
DOCMAX = 1024
NDOC = 4
KW = 1152
N_HEAD = 2
N_SUB = 2


def draw_q_weight(key, part):
    key = jax.random.fold_in(key, 11)
    base = jax.random.normal(key, (D, QH * HD), jnp.float32) * D ** (-0.5)
    return base.astype(jnp.bfloat16)


def draw_task_server(key, part):
    key = jax.random.fold_in(key, 23)
    full_key, pick_key, order_key = jax.random.split(key, 3)
    tok_count = TOKENS // TOK_DEV
    sub_count = GQ // HEADS_DEV
    chosen_full = jax.random.randint(full_key, (KVH,), 0, SERVERS).astype(jnp.int32)
    pick_keys = jax.random.split(pick_key, KVH * SERVERS)
    pick_keys = pick_keys.reshape((KVH, SERVERS) + pick_keys.shape[1:])
    order_keys = jax.random.split(order_key, KVH * SERVERS)
    order_keys = order_keys.reshape((KVH, SERVERS) + order_keys.shape[1:])

    def one_source(pick_one, order_one, chosen):
        others = jax.random.permutation(pick_one, SERVERS - 1).astype(jnp.int32)
        others = others + (others >= chosen).astype(jnp.int32)
        picks = jnp.concatenate([chosen[None], others[:TASKS - 1]])
        return picks[jax.random.permutation(order_one, TASKS)]

    def one_group(pick_row, order_row, chosen):
        return jax.vmap(one_source, (0, 0, None))(pick_row, order_row, chosen)
    table = jax.vmap(one_group)(pick_keys, order_keys, chosen_full)
    table = table.reshape(KVH, tok_count, sub_count, BLK_DEV, HEADS_DEV).transpose(1, 3, 0, 2, 4)
    return table.reshape(NBLK, QH).astype(jnp.int32)


def strengthened(array, rng, source, target, shards_of, factor):
    def block_of(dim):
        return (jnp.arange(array.shape[dim]) // (array.shape[dim] // shards_of)).reshape((-1,) + (1,) * (array.ndim - 1 - dim))

    first = jax.random.permutation(rng, shards_of)[block_of(target)]
    second = (block_of(target) + shards_of // 2) % shards_of
    return jnp.where((block_of(source) == first) | (block_of(source) == second), factor * array, array)


def block_scale(rng, dims, cuts, smallest, largest):
    def one(axis_at, shards_of):
        steps = jax.random.uniform(jax.random.fold_in(jax.random.fold_in(rng, 6), axis_at), (shards_of,), jnp.float32, smallest / len(cuts), largest / len(cuts))
        return jnp.repeat(jnp.exp(steps), dims[axis_at] // shards_of).reshape((-1,) + (1,) * (len(dims) - axis_at - 1))

    factor_of = one(*cuts[0])
    for cut in cuts[1:]:
        factor_of = factor_of * one(*cut)
    return factor_of


def split_up(amount, total, most, skew):
    loads = [(1 << 20) // math.isqrt(rank ** skew) + 1 for rank in range(2, amount + 1)]
    rest, counts = total - most - (amount - 1), [1] * (amount - 1)
    while rest > 0:
        movable = [i for i in range(amount - 1) if counts[i] < most]
        mass, budget = sum([loads[i] for i in movable]), rest
        for i in movable:
            addition = min(most - counts[i], max(1, budget * loads[i] // mass), rest)
            counts[i] = counts[i] + addition
            rest = rest - addition
    return np.array([most] + counts)


def ragged(own_key, amount, total, reach, lean):
    if amount == 2:
        one = jax.random.randint(own_key, (), max(1, total - reach), min(reach, total - 1) + 1)
        return jnp.stack([one, total - one])
    lengths = jnp.asarray(split_up(amount, total, reach, lean), jnp.int32)
    pairs = (amount - 1) // 2
    giver, taker = lengths[1:1 + 2 * pairs:2], lengths[2:2 + 2 * pairs:2]
    room = jnp.minimum(giver - 1, reach - taker)
    shifted = jax.random.randint(jax.random.fold_in(own_key, 1), (pairs,), 0, 1 << 20) % (room + 1)
    lengths = lengths.at[1:1 + 2 * pairs:2].set(giver - shifted).at[2:2 + 2 * pairs:2].set(taker + shifted)
    return lengths[jax.random.permutation(jax.random.fold_in(own_key, 2), amount)]


def scatter_about(rng, shape, width, reach, cuts=(), kind=jnp.bfloat16):
    result = width * jax.random.normal(rng, shape, jnp.float32)
    if cuts:
        result = result * block_scale(rng, shape, cuts, -0.22, 0.18)
    return jnp.clip(result, -reach, reach).astype(kind)


def noise_with(key, shape, scale, reach, cuts, heavy, held_as=jnp.bfloat16):
    entries = scale * jax.random.normal(key, shape, jnp.float32)
    if cuts:
        entries = entries * block_scale(key, shape, cuts, -0.22, 0.18)
    return jnp.clip(strengthened(entries, jax.random.fold_in(key, 3), *heavy), -reach, reach).astype(held_as)


def setup_inputs(seed: int = 0, part: int = 0) -> dict:
    key_of = jax.random.split(jax.random.key(seed), 8)
    own_keys = jax.random.split(jax.random.fold_in(key_of[7], part), 8)
    return {
        "hidden_in": scatter_about(own_keys[0], (TOKENS, D), 1.0, 6.0, ((0, 4),)),
        "norm_gain": jnp.clip(1.0 + 0.18 * jax.random.normal(key_of[1], (D,), jnp.float32), 0.099609375, 1.8984375).astype(jnp.bfloat16),
        "q_weight": draw_q_weight(jax.random.fold_in(key_of[7], 71), part),
        "kv_weight": scatter_about(key_of[3], (D, KVH * 2 * HD), D ** -0.5, 0.09375, ((0, 4), (1, 4))),
        "o_weight": noise_with(key_of[4], (QH * HD, D), (QH * HD) ** -0.5, 0.25, ((0, 4), (1, 4)), (0, 1, 4, 2.0)),
        "doc_lengths": ragged(own_keys[5], NDOC, TOKENS, DOCMAX, 2).astype(jnp.int32),
        "task_server": draw_task_server(jax.random.fold_in(jax.random.fold_in(key_of[7], part), 71), part),
    }


rope_base = 500000.0
norm_eps = 1e-05
masked_score = -1e+30

def rotate(values_in, positions):
    head_width = values_in.shape[-1]
    half_width = head_width // 2
    frequencies = rope_base ** (-(jnp.arange(half_width, dtype=jnp.float32) * 2.0 / head_width))
    angles = positions.astype(jnp.float32)[:, None] * frequencies[None, :]
    cosine = jnp.concatenate([jnp.cos(angles), jnp.cos(angles)], axis=-1)[:, None, :]
    sine_part = jnp.concatenate([jnp.sin(angles), jnp.sin(angles)], axis=-1)[:, None, :]
    turned = jnp.concatenate([-values_in[..., half_width:], values_in[..., :half_width]], axis=-1)
    return values_in * cosine + turned * sine_part

def document_start(positions, doc_lengths):
    doc_ends = jnp.cumsum(doc_lengths)
    doc_starts = doc_ends - doc_lengths
    inside = doc_starts[None, :] <= positions[:, None]
    return lax.optimization_barrier(jnp.max(jnp.where(inside, doc_starts[None, :], 0), axis=1)).astype(jnp.int32)

def reference(hidden_in, norm_gain, q_weight, kv_weight, o_weight, doc_lengths, task_server):
    hidden_float = hidden_in.astype(jnp.float32)
    mean_square = lax.optimization_barrier(jnp.mean(hidden_float * hidden_float, axis=-1, keepdims=True))
    normed = (hidden_float * lax.rsqrt(mean_square + norm_eps) * norm_gain.astype(jnp.float32)).astype(jnp.bfloat16)
    token_pos = jnp.arange(TOKENS, dtype=jnp.int32)
    token_start = document_start(token_pos, doc_lengths)
    relative = token_pos - token_start
    q_full = jnp.dot(normed, q_weight, preferred_element_type=jnp.float32).reshape(TOKENS, QH, HD)
    queries = rotate(q_full, relative).astype(jnp.bfloat16)
    kv_full = jnp.dot(normed, kv_weight, preferred_element_type=jnp.float32).reshape(TOKENS, KVH, 2, HD)
    keys = rotate(kv_full[:, :, 0], relative).astype(jnp.bfloat16)
    values = kv_full[:, :, 1].astype(jnp.bfloat16)

    def one_block(block_index):
        top_row = (block_index * BLOCK).astype(jnp.int32)
        anchor = jnp.clip(top_row + BLOCK - KW, 0, TOKENS - KW).astype(jnp.int32)
        block_q = lax.dynamic_slice_in_dim(queries, top_row, BLOCK, 0).astype(jnp.float32).reshape(BLOCK, KVH, GQ, HD)
        key_win = lax.dynamic_slice_in_dim(keys, anchor, KW, 0).astype(jnp.float32)
        value_win = lax.dynamic_slice_in_dim(values, anchor, KW, 0).astype(jnp.float32)
        scores = jnp.einsum('qhgd,khd->hgqk', block_q, key_win) * HD ** (-0.5)
        query_pos = top_row + jnp.arange(BLOCK, dtype=jnp.int32)
        query_start = lax.dynamic_slice_in_dim(token_start, top_row, BLOCK, 0)
        key_pos = anchor + jnp.arange(KW, dtype=jnp.int32)
        allowed = (key_pos[None, :] >= query_start[:, None]) & (key_pos[None, :] <= query_pos[:, None])
        peak = lax.optimization_barrier(jnp.max(jnp.where(allowed, scores, masked_score), axis=-1))
        weights = jnp.where(allowed, jnp.exp(scores - peak[..., None]), 0.0)
        denom = lax.optimization_barrier(jnp.sum(weights, axis=-1))
        probs = lax.optimization_barrier(weights.astype(jnp.bfloat16)).astype(jnp.float32)
        mixed = jnp.einsum('hgqk,khd->qhgd', probs, value_win) / jnp.transpose(denom, (2, 0, 1))[..., None]
        spread = (peak + jnp.log(denom)).reshape(QH, BLOCK)
        return (mixed.astype(jnp.bfloat16).reshape(BLOCK, QH * HD), spread)
    mixed_all, spread_all = lax.map(one_block, jnp.arange(NBLK, dtype=jnp.int32))
    attention = mixed_all.reshape(TOKENS, QH * HD)
    shares = N_HEAD * N_SUB
    share_cols = QH * HD // shares

    def add_share(share_index, running):
        start_col = (share_index * share_cols).astype(jnp.int32)
        columns = lax.dynamic_slice_in_dim(attention, start_col, share_cols, 1)
        weight_rows = lax.dynamic_slice_in_dim(o_weight, start_col, share_cols, 0)
        term = jnp.dot(columns, weight_rows, preferred_element_type=jnp.float32).astype(jnp.bfloat16)
        term = lax.optimization_barrier(term)
        return running + term.astype(jnp.float32)
    projected = lax.fori_loop(0, shares, add_share, jnp.zeros((TOKENS, D), jnp.float32))
    layer_out = (hidden_float + projected).astype(jnp.bfloat16)
    block_ids = jnp.broadcast_to(jnp.arange(NBLK, dtype=jnp.int32)[:, None], (NBLK, QH))
    head_ids = jnp.broadcast_to(jnp.arange(QH, dtype=jnp.int32)[None, :], (NBLK, QH))
    source_ids = block_ids // BLK_DEV * N_SUB + head_ids % GQ // HEADS_DEV
    group_ids = head_ids // GQ
    task_lse = jnp.zeros((SERVERS, SERVERS, KVH, BLOCK), jnp.float32)
    task_lse = task_lse.at[task_server, source_ids, group_ids].set(spread_all)
    return (layer_out, task_lse)
```

```python
import functools

import jax
import jax.numpy as jnp
from jax import lax
from jax.experimental import pallas as pl
from jax.experimental.pallas import tpu as pltpu
from jax.sharding import PartitionSpec as P

BLOCK = 128
HEAD = 128
DOCMAX = 1024
rope_base = 500000.0
norm_eps = 1e-05
masked_score = -1e30
MESH = pl.DeviceIdType.MESH


def kernel(
    sizes,
    doc_ref,
    table_ref,
    hid_ref,
    gain_ref,
    freq_ref,
    q_ref,
    kv_ref,
    o_ref,
    out_ref,
    lse_ref,
    hid,
    normed,
    qw,
    kvw,
    o_stage,
    wo,
    q_acc,
    kv_acc,
    cos_buf,
    sin_buf,
    queries,
    window,
    att,
    lse_mine,
    lse_all,
    loc_sem,
    z_send,
    z_recv,
    y_send,
    y_recv,
    o_send,
    o_recv,
    k_send,
    k_recv,
    kc_send,
    kc_recv,
    a_send,
    a_recv,
    ac_send,
    ac_recv,
    l_send,
    l_recv,
):
    groups, toks, heads, subs = sizes
    y = lax.axis_index("group")
    t = lax.axis_index("tok")
    x = lax.axis_index("head")
    c = lax.axis_index("sub")
    rows, width = hid.shape
    depth = q_ref.shape[0]
    half = depth // 2
    o_half = o_ref.shape[0] // 2
    shares = heads * subs
    mine = x * subs + c
    blocks = rows // BLOCK
    heads_here = q_ref.shape[1] // HEAD
    back = DOCMAX // rows
    docs = doc_ref.shape[0]
    tasks = blocks * heads_here
    sent = []

    def at_half(ref, index, size):
        return ref.at[pl.ds(pl.multiple_of(index * size, size), size)]

    def when(cond, fn):
        if cond is True:
            fn()
        else:
            pl.when(cond)(fn)

    def send(cond, src, dst, send_sem, recv_sem, device):
        copy = pltpu.make_async_remote_copy(
            src_ref=src,
            dst_ref=dst,
            send_sem=send_sem,
            recv_sem=recv_sem,
            device_id=device,
            device_id_type=MESH,
        )
        when(cond, copy.start)
        sent.append((cond, copy))

    def arrived(cond, dst, sem):
        when(cond, pltpu.make_async_copy(dst, dst, sem).wait)

    load_hid = pltpu.make_async_copy(hid_ref, hid, loc_sem.at[0])
    load_q = pltpu.make_async_copy(q_ref, qw.at[t], loc_sem.at[1])
    load_kv = pltpu.make_async_copy(kv_ref, kvw.at[t], loc_sem.at[2])
    load_hid.start()
    load_q.start()
    load_kv.start()

    barrier = pltpu.get_barrier_semaphore()
    count = 0
    for dy in range(groups):
        for dx in range(heads):
            for dc in range(subs):
                if dy or dx or dc:
                    pl.semaphore_signal(
                        barrier,
                        inc=1,
                        device_id=(
                            lax.rem(y + dy, groups),
                            t,
                            lax.rem(x + dx, heads),
                            lax.rem(c + dc, subs),
                        ),
                        device_id_type=MESH,
                    )
                    count += 1
    for dt in range(1, toks):
        for dc in range(subs):
            pl.semaphore_signal(
                barrier,
                inc=1,
                device_id=(y, lax.rem(t + dt, toks), x, lax.rem(c + dc, subs)),
                device_id_type=MESH,
            )
            count += 1
    pl.semaphore_wait(barrier, count)

    slots = (qw, kvw, o_stage)

    def piece(array, shard):
        if array == 2:
            return o_stage.at[shard]
        return at_half(slots[array].at[shard], y, half)

    def pass_on(array, shard, cond, src, direction):
        target = t + (1 if direction == 0 else -1)
        inside = (target < toks) if direction == 0 else (target >= 0)
        send(
            cond & inside,
            src,
            piece(array, shard),
            z_send.at[array, direction, shard],
            z_recv.at[array, shard],
            (y, target, x, c),
        )

    def spread_o(shard, cond, src):
        dest_x, dest_c = shard // subs, lax.rem(shard, subs)
        dst = wo.at[mine, pl.ds(pl.multiple_of(y * o_half, o_half), o_half)]
        for dy in range(groups):
            dest_y = lax.rem(y + dy, groups)
            remote = cond if dy else cond & (shard != mine)
            send(
                remote,
                src,
                dst,
                o_send.at[shard, dy],
                o_recv.at[mine, y],
                (dest_y, t, dest_x, dest_c),
            )
        when(
            cond & (shard == mine),
            pltpu.make_async_copy(src, dst, o_recv.at[mine, y]).start,
        )

    yes = t >= 0
    own = (at_half(q_ref, y, half), at_half(kv_ref, y, half), at_half(o_ref, y, o_half))
    for array in range(2):
        for direction in range(2):
            pass_on(array, t, yes, own[array], direction)
    for direction in range(2):
        pass_on(2, t, yes, own[2], direction)
    spread_o(t, yes, own[2])

    load_hid.wait()
    step_rows = 64

    def norm_rows(step, carry):
        at = pl.ds(pl.multiple_of(step * step_rows, step_rows), step_rows)
        part = hid[at, :].astype(jnp.float32)
        scale = lax.rsqrt(jnp.mean(part * part, axis=-1, keepdims=True) + norm_eps)
        result = (part * scale * gain_ref[...].astype(jnp.float32)).astype(jnp.bfloat16)
        for shard in range(toks):
            for side in range(2):
                first = shard * depth + side * half
                normed[shard, side, at, :] = result[:, first : first + half]
        return carry

    lax.fori_loop(0, rows // step_rows, norm_rows, 0)

    def doc_start(pos):
        start = jnp.zeros_like(pos)
        total = doc_ref[0] * 0
        for doc in range(docs):
            start = jnp.where(total <= pos, total, start)
            total = total + doc_ref[doc]
        return start

    def angles(step, carry):
        at = pl.ds(pl.multiple_of(step * BLOCK, BLOCK), BLOCK)
        pos = t * rows + step * BLOCK + lax.broadcasted_iota(jnp.int32, (BLOCK, HEAD), 0)
        angle = (pos - doc_start(pos)).astype(jnp.float32) * freq_ref[...]
        cos_buf[at, :] = jnp.cos(angle)
        sign = jnp.where(lax.broadcasted_iota(jnp.int32, (BLOCK, HEAD), 1) < HEAD // 2, -1.0, 1.0)
        sin_buf[at, :] = jnp.sin(angle) * sign
        return carry

    lax.fori_loop(0, blocks, angles, 0)

    def project(shard, side, first=False):
        at = pl.ds(pl.multiple_of(side * half, half), half)
        part = normed[shard, side]
        q_part = jnp.dot(part, qw[shard, at, :], preferred_element_type=jnp.float32)
        kv_part = jnp.dot(part, kvw[shard, at, :], preferred_element_type=jnp.float32)
        if first:
            q_acc[...] = q_part
            kv_acc[...] = kv_part
        else:
            q_acc[...] += q_part
            kv_acc[...] += kv_part

    load_q.wait()
    load_kv.wait()
    project(t, 0, first=True)
    project(t, 1)

    other = lax.rem(y + 1, groups)
    for k in range(1, toks):
        for direction in range(2):
            shard = t - k if direction == 0 else t + k
            valid = (shard >= 0) if direction == 0 else (shard < toks)
            for array in range(2):
                arrived(valid, piece(array, shard), z_recv.at[array, shard])
                pass_on(array, shard, valid, piece(array, shard), direction)
                send(
                    valid,
                    piece(array, shard),
                    piece(array, shard),
                    y_send.at[array, shard],
                    y_recv.at[array, shard],
                    (other, t, x, c),
                )
        for direction in range(2):
            shard = t - k if direction == 0 else t + k
            valid = (shard >= 0) if direction == 0 else (shard < toks)
            pl.when(valid)(functools.partial(project, shard, y))
    for k in range(1, toks):
        for direction in range(2):
            shard = t - k if direction == 0 else t + k
            valid = (shard >= 0) if direction == 0 else (shard < toks)
            arrived(valid, o_stage.at[shard], z_recv.at[2, shard])
            pass_on(2, shard, valid, o_stage.at[shard], direction)
            spread_o(shard, valid, o_stage.at[shard])
            for array in range(2):
                arrived(
                    valid, at_half(slots[array].at[shard], other, half), y_recv.at[array, shard]
                )
            pl.when(valid)(functools.partial(project, shard, other))

    def rotated(u):
        return u * cos_buf[...] + pltpu.roll(u, HEAD // 2, 1) * sin_buf[...]

    kv_raw = kv_acc[...]
    own_rows = pl.ds(back * rows, rows)
    window[c, own_rows, :] = jnp.where(c == 0, rotated(kv_raw), kv_raw).astype(jnp.bfloat16)
    twin = lax.rem(c + 1, subs)
    for j in range(1, back + 1):
        send(
            t + j < toks,
            window.at[c, own_rows],
            window.at[c, pl.ds((back - j) * rows, rows)],
            k_send.at[j - 1],
            k_recv.at[j - 1],
            (y, t + j, x, c),
        )
    send(
        True,
        window.at[c, own_rows],
        window.at[c, own_rows],
        kc_send.at[0],
        kc_recv.at[0],
        (y, t, x, twin),
    )
    for h in range(heads_here):
        turned = rotated(q_acc[:, h * HEAD : (h + 1) * HEAD]).astype(jnp.bfloat16)
        for b in range(blocks):
            queries[b, h * BLOCK : (h + 1) * BLOCK, :] = turned[b * BLOCK : (b + 1) * BLOCK]
    for j in range(1, back + 1):
        at = pl.ds((back - j) * rows, rows)

        def blank(at=at):
            window[:, at, :] = jnp.zeros((2, rows, HEAD), jnp.bfloat16)

        pl.when(t < j)(blank)
        arrived(t >= j, window.at[c, at], k_recv.at[j - 1])
        send(
            t >= j,
            window.at[c, at],
            window.at[c, at],
            kc_send.at[j],
            kc_recv.at[j],
            (y, t, x, twin),
        )
    arrived(True, window.at[twin, own_rows], kc_recv.at[0])
    for j in range(1, back + 1):
        at = pl.ds((back - j) * rows, rows)
        arrived(t >= j, window.at[twin, at], kc_recv.at[j])

    reach = DOCMAX + BLOCK
    stack = heads_here * BLOCK
    scale = HEAD ** (-0.5)
    diagonal = lax.broadcasted_iota(jnp.int32, (BLOCK, BLOCK), 0) == lax.broadcasted_iota(
        jnp.int32, (BLOCK, BLOCK), 1
    )
    for b in range(blocks):
        keys = window[0, b * BLOCK : b * BLOCK + reach, :]
        values = window[1, b * BLOCK : b * BLOCK + reach, :]
        scores = (
            lax.dot_general(
                queries[b], keys, (((1,), (1,)), ((), ())), preferred_element_type=jnp.float32
            )
            * scale
        )
        row = lax.broadcasted_iota(jnp.int32, (stack, 1), 0)
        pos = t * rows + b * BLOCK + lax.rem(row, BLOCK)
        start = doc_start(pos)
        key_pos = (t - back) * rows + b * BLOCK + lax.broadcasted_iota(jnp.int32, (1, reach), 1)
        allowed = (key_pos >= start) & (key_pos <= pos)
        scores = jnp.where(allowed, scores, masked_score)
        peak = jnp.max(scores, axis=-1, keepdims=True)
        weights = jnp.exp(scores - peak)
        denom = jnp.sum(weights, axis=-1, keepdims=True)
        mixed = jnp.dot(weights.astype(jnp.bfloat16), values, preferred_element_type=jnp.float32)
        mixed = (mixed / denom).astype(jnp.bfloat16)
        spread = peak + jnp.log(denom)
        for h in range(heads_here):
            att[mine, b, :, h * HEAD : (h + 1) * HEAD] = mixed[h * BLOCK : (h + 1) * BLOCK]
            lse_mine[pl.ds(b * heads_here + h, 1), :] = jnp.sum(
                jnp.where(diagonal, spread[h * BLOCK : (h + 1) * BLOCK], 0.0),
                axis=0,
                keepdims=True,
            )
        for dx in range(1, heads):
            send(
                True,
                att.at[mine, b],
                att.at[mine, b],
                a_send.at[dx, b],
                a_recv.at[x, b],
                (y, t, lax.rem(x + dx, heads), c),
            )
        send(
            True,
            att.at[mine, b],
            att.at[mine, b],
            ac_send.at[0, b],
            ac_recv.at[x, b],
            (y, t, x, twin),
        )

    me = t * subs + c
    for dt in range(toks):
        for dc in range(subs):
            if dt or dc:
                send(
                    True,
                    lse_mine,
                    lse_all.at[me],
                    l_send.at[dt * subs + dc],
                    l_recv.at[me],
                    (y, lax.rem(t + dt, toks), x, lax.rem(c + dc, subs)),
                )
    lse_all[me] = lse_mine[...]

    for r in range(shares):
        for side in range(2):
            dst = wo.at[r, pl.ds(side * o_half, o_half)]
            arrived(True, dst, o_recv.at[r, side])
    share_cols = out_ref.shape[1]
    columns = pl.ds(pl.multiple_of(mine * share_cols, share_cols), share_cols)
    for b in range(blocks):
        for dx in range(1, heads):
            source = lax.rem(x + dx, heads)
            arrived(True, att.at[source * subs + c, b], a_recv.at[source, b])
            send(
                True,
                att.at[source * subs + c, b],
                att.at[source * subs + c, b],
                ac_send.at[dx, b],
                ac_recv.at[source, b],
                (y, t, x, twin),
            )
    for b in range(blocks):
        for dx in range(heads):
            source = lax.rem(x + dx, heads)
            arrived(True, att.at[source * subs + twin, b], ac_recv.at[source, b])
        at = slice(b * BLOCK, (b + 1) * BLOCK)
        summed = jnp.zeros((BLOCK, share_cols), jnp.float32)
        for r in range(shares):
            summed += (
                jnp.dot(att[r, b], wo[r], preferred_element_type=jnp.float32)
                .astype(jnp.bfloat16)
                .astype(jnp.float32)
            )
        out_ref[at, :] = (hid[at, columns].astype(jnp.float32) + summed).astype(jnp.bfloat16)

    group_heads = heads_here * subs
    for dt in range(toks):
        for dc in range(subs):
            source = lax.rem(t + dt, toks) * subs + lax.rem(c + dc, subs)
            if dt or dc:
                arrived(True, lse_all.at[source], l_recv.at[source])
    for source in range(toks * subs):
        kept = jnp.zeros((1, BLOCK), jnp.float32)
        for task in range(tasks):
            server = table_ref[
                (source // subs) * blocks + task // heads_here,
                x * group_heads + (source % subs) * heads_here + task % heads_here,
            ]
            kept = kept + jnp.where(server == me, lse_all[source, task : task + 1, :], 0.0)
        lse_ref[source : source + 1, :] = kept

    for cond, copy in sent:
        when(cond, copy.wait_send)


def body(sizes, hidden_in, norm_gain, q_weight, kv_weight, o_weight, doc_lengths, task_server):
    groups, toks, heads, subs = sizes
    rows, width = hidden_in.shape
    depth, q_cols = q_weight.shape
    o_rows, o_cols = o_weight.shape
    shares = heads * subs
    assert groups == 2 and subs == 2 and toks == shares
    assert width // shares == o_cols and DOCMAX % rows == 0
    blocks = rows // BLOCK
    heads_here = q_cols // HEAD
    back = DOCMAX // rows
    tasks = blocks * heads_here
    servers = toks * subs
    half = jnp.arange(HEAD // 2, dtype=jnp.float32)
    freq = rope_base ** (-(half * 2.0 / HEAD))
    freq = jnp.concatenate([freq, freq])[None, :]
    bf16, f32 = jnp.bfloat16, jnp.float32
    dma = pltpu.SemaphoreType.DMA
    any_spec = pl.BlockSpec(memory_space=pl.ANY)
    vmem = pl.BlockSpec(memory_space=pltpu.VMEM)
    smem = pl.BlockSpec(memory_space=pltpu.SMEM)
    layer_out, lse = pl.pallas_call(
        functools.partial(kernel, sizes),
        out_shape=(
            jax.ShapeDtypeStruct((rows, o_cols), bf16),
            jax.ShapeDtypeStruct((servers, BLOCK), f32),
        ),
        in_specs=[smem, smem, any_spec, vmem, vmem, any_spec, any_spec, any_spec],
        out_specs=(vmem, vmem),
        scratch_shapes=[
            pltpu.VMEM((rows, width), bf16),
            pltpu.VMEM((toks, 2, rows, depth // 2), bf16),
            pltpu.VMEM((toks, depth, q_cols), bf16),
            pltpu.VMEM((toks, depth, HEAD), bf16),
            pltpu.VMEM((toks, o_rows // 2, o_cols), bf16),
            pltpu.VMEM((shares, o_rows, o_cols), bf16),
            pltpu.VMEM((rows, q_cols), f32),
            pltpu.VMEM((rows, HEAD), f32),
            pltpu.VMEM((rows, HEAD), f32),
            pltpu.VMEM((rows, HEAD), f32),
            pltpu.VMEM((blocks, heads_here * BLOCK, HEAD), bf16),
            pltpu.VMEM((2, (back + 1) * rows, HEAD), bf16),
            pltpu.VMEM((shares, blocks, BLOCK, q_cols), bf16),
            pltpu.VMEM((tasks, BLOCK), f32),
            pltpu.VMEM((servers, tasks, BLOCK), f32),
            dma((3,)),
            dma((3, 2, toks)),
            dma((3, toks)),
            dma((2, toks)),
            dma((2, toks)),
            dma((toks, groups)),
            dma((shares, 2)),
            dma((back,)),
            dma((back,)),
            dma((back + 1,)),
            dma((back + 1,)),
            dma((heads, blocks)),
            dma((heads, blocks)),
            dma((heads, blocks)),
            dma((heads, blocks)),
            dma((servers,)),
            dma((servers,)),
        ],
        compiler_params=pltpu.CompilerParams(
            collective_id=0, has_side_effects=True, vmem_limit_bytes=56 * 1024 * 1024
        ),
        cost_estimate=pl.CostEstimate(
            flops=4 * 10**9, bytes_accessed=8 * 2**20, transcendentals=2 * 10**6
        ),
    )(
        doc_lengths,
        task_server,
        hidden_in,
        norm_gain[None, :],
        freq,
        q_weight,
        kv_weight,
        o_weight,
    )
    return (layer_out, lse.reshape(1, servers, 1, BLOCK))


def solution(mesh):
    placed = (
        P(("group", "tok"), None),
        P(),
        P("tok", ("head", "sub")),
        P("tok", ("head", "sub")),
        P(("head", "sub"), "tok"),
        P("group"),
        P("group", None),
    )
    sizes = tuple(mesh.shape[name] for name in ("group", "tok", "head", "sub"))
    return jax.shard_map(
        functools.partial(body, sizes),
        mesh=mesh,
        in_specs=placed,
        out_specs=(
            P(("group", "tok"), ("head", "sub")),
            P(("group", "tok", "sub"), None, "head", None),
        ),
        check_vma=False,
    )
```

```python
import functools

import jax
import jax.numpy as jnp
from jax import lax
from jax.experimental import pallas as pl
from jax.experimental.pallas import tpu as pltpu
from jax.sharding import PartitionSpec as P

BLOCK = 128
HEAD = 128
DOCMAX = 1024
rope_base = 500000.0
norm_eps = 1e-05
masked_score = -1e30
MESH = pl.DeviceIdType.MESH


def kernel(
    sizes,
    doc_ref,
    table_ref,
    hid_ref,
    gain_ref,
    freq_ref,
    q_ref,
    kv_ref,
    o_ref,
    out_ref,
    lse_ref,
    hid,
    normed,
    qw,
    kvw,
    o_stage,
    wo,
    q_acc,
    kv_acc,
    cos_buf,
    sin_buf,
    queries,
    window,
    att,
    lse_mine,
    lse_all,
    loc_sem,
    z_send,
    z_recv,
    y_send,
    y_recv,
    o_send,
    o_recv,
    k_send,
    k_recv,
    kc_send,
    kc_recv,
    a_send,
    a_recv,
    ac_send,
    ac_recv,
    l_send,
    l_recv,
):
    groups, toks, heads, subs = sizes
    y = lax.axis_index("group")
    t = lax.axis_index("tok")
    x = lax.axis_index("head")
    c = lax.axis_index("sub")
    rows, width = hid.shape
    depth = q_ref.shape[0]
    half = depth // 2
    o_half = o_ref.shape[0] // 2
    shares = heads * subs
    mine = x * subs + c
    blocks = rows // BLOCK
    heads_here = q_ref.shape[1] // HEAD
    back = DOCMAX // rows
    docs = doc_ref.shape[0]
    tasks = blocks * heads_here
    sent = []

    def at_half(ref, index, size):
        return ref.at[pl.ds(pl.multiple_of(index * size, size), size)]

    def when(cond, fn):
        if cond is True:
            fn()
        else:
            pl.when(cond)(fn)

    def send(cond, src, dst, send_sem, recv_sem, device):
        copy = pltpu.make_async_remote_copy(
            src_ref=src,
            dst_ref=dst,
            send_sem=send_sem,
            recv_sem=recv_sem,
            device_id=device,
            device_id_type=MESH,
        )
        when(cond, copy.start)
        sent.append((cond, copy))

    def arrived(cond, dst, sem):
        when(cond, pltpu.make_async_copy(dst, dst, sem).wait)

    load_hid = pltpu.make_async_copy(hid_ref, hid, loc_sem.at[0])
    load_q = pltpu.make_async_copy(q_ref, qw.at[t], loc_sem.at[1])
    load_kv = pltpu.make_async_copy(kv_ref, kvw.at[t], loc_sem.at[2])
    load_hid.start()
    load_q.start()
    load_kv.start()

    barrier = pltpu.get_barrier_semaphore()
    count = 0
    for dy in range(groups):
        for dx in range(heads):
            for dc in range(subs):
                if dy or dx or dc:
                    pl.semaphore_signal(
                        barrier,
                        inc=1,
                        device_id=(
                            lax.rem(y + dy, groups),
                            t,
                            lax.rem(x + dx, heads),
                            lax.rem(c + dc, subs),
                        ),
                        device_id_type=MESH,
                    )
                    count += 1
    for dt in range(1, toks):
        for dc in range(subs):
            pl.semaphore_signal(
                barrier,
                inc=1,
                device_id=(y, lax.rem(t + dt, toks), x, lax.rem(c + dc, subs)),
                device_id_type=MESH,
            )
            count += 1
    pl.semaphore_wait(barrier, count)

    slots = (qw, kvw, o_stage)

    def piece(array, shard):
        if array == 2:
            return o_stage.at[shard]
        return at_half(slots[array].at[shard], y, half)

    def pass_on(array, shard, cond, src, direction):
        target = t + (1 if direction == 0 else -1)
        inside = (target < toks) if direction == 0 else (target >= 0)
        send(
            cond & inside,
            src,
            piece(array, shard),
            z_send.at[array, direction, shard],
            z_recv.at[array, shard],
            (y, target, x, c),
        )

    def spread_o(shard, cond, src):
        dest_x, dest_c = shard // subs, lax.rem(shard, subs)
        dst = wo.at[mine, pl.ds(pl.multiple_of(y * o_half, o_half), o_half)]
        for dy in range(groups):
            dest_y = lax.rem(y + dy, groups)
            remote = cond if dy else cond & (shard != mine)
            send(
                remote,
                src,
                dst,
                o_send.at[shard, dy],
                o_recv.at[mine, y],
                (dest_y, t, dest_x, dest_c),
            )
        when(
            cond & (shard == mine),
            pltpu.make_async_copy(src, dst, o_recv.at[mine, y]).start,
        )

    yes = t >= 0
    own = (at_half(q_ref, y, half), at_half(kv_ref, y, half), at_half(o_ref, y, o_half))
    for array in range(2):
        for direction in range(2):
            pass_on(array, t, yes, own[array], direction)

    load_hid.wait()
    step_rows = 64

    def norm_rows(step, carry):
        at = pl.ds(pl.multiple_of(step * step_rows, step_rows), step_rows)
        part = hid[at, :].astype(jnp.float32)
        scale = lax.rsqrt(jnp.mean(part * part, axis=-1, keepdims=True) + norm_eps)
        result = (part * scale * gain_ref[...].astype(jnp.float32)).astype(jnp.bfloat16)
        for shard in range(toks):
            for side in range(2):
                first = shard * depth + side * half
                normed[shard, side, at, :] = result[:, first : first + half]
        return carry

    lax.fori_loop(0, rows // step_rows, norm_rows, 0)

    def doc_start(pos):
        start = jnp.zeros_like(pos)
        total = doc_ref[0] * 0
        for doc in range(docs):
            start = jnp.where(total <= pos, total, start)
            total = total + doc_ref[doc]
        return start

    def angles(step, carry):
        at = pl.ds(pl.multiple_of(step * BLOCK, BLOCK), BLOCK)
        pos = t * rows + step * BLOCK + lax.broadcasted_iota(jnp.int32, (BLOCK, HEAD), 0)
        angle = (pos - doc_start(pos)).astype(jnp.float32) * freq_ref[...]
        cos_buf[at, :] = jnp.cos(angle)
        sign = jnp.where(lax.broadcasted_iota(jnp.int32, (BLOCK, HEAD), 1) < HEAD // 2, -1.0, 1.0)
        sin_buf[at, :] = jnp.sin(angle) * sign
        return carry


    def project(shard, side, first=False):
        at = pl.ds(pl.multiple_of(side * half, half), half)
        part = normed[shard, side]
        q_part = jnp.dot(part, qw[shard, at, :], preferred_element_type=jnp.float32)
        kv_part = jnp.dot(part, kvw[shard, at, :], preferred_element_type=jnp.float32)
        if first:
            q_acc[...] = q_part
            kv_acc[...] = kv_part
        else:
            q_acc[...] += q_part
            kv_acc[...] += kv_part

    other = lax.rem(y + 1, groups)

    def from_step(k, direction):
        shard = t - k if direction == 0 else t + k
        return shard, (shard >= 0) if direction == 0 else (shard < toks)

    def other_halves(k):
        for direction in range(2):
            shard, valid = from_step(k, direction)
            for array in range(2):
                arrived(
                    valid, at_half(slots[array].at[shard], other, half), y_recv.at[array, shard]
                )
            pl.when(valid)(functools.partial(project, shard, other))

    def chain_o(k):
        for direction in range(2):
            shard, valid = from_step(k, direction)
            arrived(valid, o_stage.at[shard], z_recv.at[2, shard])
            pass_on(2, shard, valid, o_stage.at[shard], direction)
            spread_o(shard, valid, o_stage.at[shard])

    for k in range(1, toks):
        for direction in range(2):
            shard, valid = from_step(k, direction)
            for array in range(2):
                arrived(valid, piece(array, shard), z_recv.at[array, shard])
                pass_on(array, shard, valid, piece(array, shard), direction)
                send(
                    valid,
                    piece(array, shard),
                    piece(array, shard),
                    y_send.at[array, shard],
                    y_recv.at[array, shard],
                    (other, t, x, c),
                )
        if k == max(toks - 2, 1):
            for direction in range(2):
                pass_on(2, t, yes, own[2], direction)
            spread_o(t, yes, own[2])
        if k == 1:
            lax.fori_loop(0, blocks, angles, 0)
            load_q.wait()
            load_kv.wait()
            project(t, 0, first=True)
            project(t, 1)
        else:
            other_halves(k - 1)
        for direction in range(2):
            shard, valid = from_step(k, direction)
            pl.when(valid)(functools.partial(project, shard, y))
    other_halves(toks - 1)

    def rotated(u):
        return u * cos_buf[...] + pltpu.roll(u, HEAD // 2, 1) * sin_buf[...]

    kv_raw = kv_acc[...]
    own_rows = pl.ds(back * rows, rows)
    window[c, own_rows, :] = jnp.where(c == 0, rotated(kv_raw), kv_raw).astype(jnp.bfloat16)
    twin = lax.rem(c + 1, subs)
    for j in range(1, back + 1):
        send(
            t + j < toks,
            window.at[c, own_rows],
            window.at[c, pl.ds((back - j) * rows, rows)],
            k_send.at[j - 1],
            k_recv.at[j - 1],
            (y, t + j, x, c),
        )
    send(
        True,
        window.at[c, own_rows],
        window.at[c, own_rows],
        kc_send.at[0],
        kc_recv.at[0],
        (y, t, x, twin),
    )
    for h in range(heads_here):
        turned = rotated(q_acc[:, h * HEAD : (h + 1) * HEAD]).astype(jnp.bfloat16)
        for b in range(blocks):
            queries[b, h * BLOCK : (h + 1) * BLOCK, :] = turned[b * BLOCK : (b + 1) * BLOCK]
    chain_o(1)
    for j in range(1, back + 1):
        at = pl.ds((back - j) * rows, rows)

        def blank(at=at):
            window[:, at, :] = jnp.zeros((2, rows, HEAD), jnp.bfloat16)

        pl.when(t < j)(blank)
        arrived(t >= j, window.at[c, at], k_recv.at[j - 1])
        send(
            t >= j,
            window.at[c, at],
            window.at[c, at],
            kc_send.at[j],
            kc_recv.at[j],
            (y, t, x, twin),
        )
    arrived(True, window.at[twin, own_rows], kc_recv.at[0])
    for j in range(1, back + 1):
        at = pl.ds((back - j) * rows, rows)
        arrived(t >= j, window.at[twin, at], kc_recv.at[j])

    reach = DOCMAX + BLOCK
    stack = heads_here * BLOCK
    scale = HEAD ** (-0.5)
    diagonal = lax.broadcasted_iota(jnp.int32, (BLOCK, BLOCK), 0) == lax.broadcasted_iota(
        jnp.int32, (BLOCK, BLOCK), 1
    )
    def forward(b):
        for dx in range(1, heads):
            source = lax.rem(x + dx, heads)
            arrived(True, att.at[source * subs + c, b], a_recv.at[source, b])
            send(
                True,
                att.at[source * subs + c, b],
                att.at[source * subs + c, b],
                ac_send.at[dx, b],
                ac_recv.at[source, b],
                (y, t, x, twin),
            )

    for b in range(blocks):
        keys = window[0, b * BLOCK : b * BLOCK + reach, :]
        values = window[1, b * BLOCK : b * BLOCK + reach, :]
        scores = (
            lax.dot_general(
                queries[b], keys, (((1,), (1,)), ((), ())), preferred_element_type=jnp.float32
            )
            * scale
        )
        row = lax.broadcasted_iota(jnp.int32, (stack, 1), 0)
        pos = t * rows + b * BLOCK + lax.rem(row, BLOCK)
        start = doc_start(pos)
        key_pos = (t - back) * rows + b * BLOCK + lax.broadcasted_iota(jnp.int32, (1, reach), 1)
        allowed = (key_pos >= start) & (key_pos <= pos)
        scores = jnp.where(allowed, scores, masked_score)
        peak = jnp.max(scores, axis=-1, keepdims=True)
        weights = jnp.exp(scores - peak)
        denom = jnp.sum(weights, axis=-1, keepdims=True)
        mixed = jnp.dot(weights.astype(jnp.bfloat16), values, preferred_element_type=jnp.float32)
        mixed = (mixed / denom).astype(jnp.bfloat16)
        spread = peak + jnp.log(denom)
        for h in range(heads_here):
            att[mine, b, :, h * HEAD : (h + 1) * HEAD] = mixed[h * BLOCK : (h + 1) * BLOCK]
            lse_mine[pl.ds(b * heads_here + h, 1), :] = jnp.sum(
                jnp.where(diagonal, spread[h * BLOCK : (h + 1) * BLOCK], 0.0),
                axis=0,
                keepdims=True,
            )
        for dx in range(1, heads):
            send(
                True,
                att.at[mine, b],
                att.at[mine, b],
                a_send.at[dx, b],
                a_recv.at[x, b],
                (y, t, lax.rem(x + dx, heads), c),
            )
        send(
            True,
            att.at[mine, b],
            att.at[mine, b],
            ac_send.at[0, b],
            ac_recv.at[x, b],
            (y, t, x, twin),
        )
        if b == 0 and toks > 2:
            chain_o(2)
        if b:
            forward(b - 1)
        if b == blocks - 2:
            for k in range(3, toks):
                chain_o(k)

    me = t * subs + c
    for dt in range(toks):
        for dc in range(subs):
            if dt or dc:
                send(
                    True,
                    lse_mine,
                    lse_all.at[me],
                    l_send.at[dt * subs + dc],
                    l_recv.at[me],
                    (y, lax.rem(t + dt, toks), x, lax.rem(c + dc, subs)),
                )
    lse_all[me] = lse_mine[...]

    for r in range(shares):
        for side in range(2):
            dst = wo.at[r, pl.ds(side * o_half, o_half)]
            arrived(True, dst, o_recv.at[r, side])
    share_cols = out_ref.shape[1]
    columns = pl.ds(pl.multiple_of(mine * share_cols, share_cols), share_cols)
    pair = 2
    for first in range(0, blocks, pair):
        if first + pair == blocks:
            forward(blocks - 1)
        for b in range(first, first + pair):
            for dx in range(heads):
                source = lax.rem(x + dx, heads)
                arrived(True, att.at[source * subs + twin, b], ac_recv.at[source, b])
        at = slice(first * BLOCK, (first + pair) * BLOCK)
        summed = jnp.zeros((pair * BLOCK, share_cols), jnp.float32)
        for r in range(shares):
            product = jnp.dot(
                att[r, first : first + pair].reshape(pair * BLOCK, att.shape[3]),
                wo[r],
                preferred_element_type=jnp.float32,
            )
            summed += product.astype(jnp.bfloat16).astype(jnp.float32)
        out_ref[at, :] = (hid[at, columns].astype(jnp.float32) + summed).astype(jnp.bfloat16)

    group_heads = heads_here * subs
    for dt in range(toks):
        for dc in range(subs):
            source = lax.rem(t + dt, toks) * subs + lax.rem(c + dc, subs)
            if dt or dc:
                arrived(True, lse_all.at[source], l_recv.at[source])
    for source in range(toks * subs):
        kept = jnp.zeros((1, BLOCK), jnp.float32)
        for task in range(tasks):
            server = table_ref[
                (source // subs) * blocks + task // heads_here,
                x * group_heads + (source % subs) * heads_here + task % heads_here,
            ]
            kept = kept + jnp.where(server == me, lse_all[source, task : task + 1, :], 0.0)
        lse_ref[source : source + 1, :] = kept

    for cond, copy in sent:
        when(cond, copy.wait_send)


def body(sizes, hidden_in, norm_gain, q_weight, kv_weight, o_weight, doc_lengths, task_server):
    groups, toks, heads, subs = sizes
    rows, width = hidden_in.shape
    depth, q_cols = q_weight.shape
    o_rows, o_cols = o_weight.shape
    shares = heads * subs
    assert groups == 2 and subs == 2 and toks == shares
    assert width // shares == o_cols and DOCMAX % rows == 0
    blocks = rows // BLOCK
    heads_here = q_cols // HEAD
    back = DOCMAX // rows
    tasks = blocks * heads_here
    servers = toks * subs
    half = jnp.arange(HEAD // 2, dtype=jnp.float32)
    freq = rope_base ** (-(half * 2.0 / HEAD))
    freq = jnp.concatenate([freq, freq])[None, :]
    bf16, f32 = jnp.bfloat16, jnp.float32
    dma = pltpu.SemaphoreType.DMA
    any_spec = pl.BlockSpec(memory_space=pl.ANY)
    vmem = pl.BlockSpec(memory_space=pltpu.VMEM)
    smem = pl.BlockSpec(memory_space=pltpu.SMEM)
    layer_out, lse = pl.pallas_call(
        functools.partial(kernel, sizes),
        out_shape=(
            jax.ShapeDtypeStruct((rows, o_cols), bf16),
            jax.ShapeDtypeStruct((servers, BLOCK), f32),
        ),
        in_specs=[smem, smem, any_spec, vmem, vmem, any_spec, any_spec, any_spec],
        out_specs=(vmem, vmem),
        scratch_shapes=[
            pltpu.VMEM((rows, width), bf16),
            pltpu.VMEM((toks, 2, rows, depth // 2), bf16),
            pltpu.VMEM((toks, depth, q_cols), bf16),
            pltpu.VMEM((toks, depth, HEAD), bf16),
            pltpu.VMEM((toks, o_rows // 2, o_cols), bf16),
            pltpu.VMEM((shares, o_rows, o_cols), bf16),
            pltpu.VMEM((rows, q_cols), f32),
            pltpu.VMEM((rows, HEAD), f32),
            pltpu.VMEM((rows, HEAD), f32),
            pltpu.VMEM((rows, HEAD), f32),
            pltpu.VMEM((blocks, heads_here * BLOCK, HEAD), bf16),
            pltpu.VMEM((2, (back + 1) * rows, HEAD), bf16),
            pltpu.VMEM((shares, blocks, BLOCK, q_cols), bf16),
            pltpu.VMEM((tasks, BLOCK), f32),
            pltpu.VMEM((servers, tasks, BLOCK), f32),
            dma((3,)),
            dma((3, 2, toks)),
            dma((3, toks)),
            dma((2, toks)),
            dma((2, toks)),
            dma((toks, groups)),
            dma((shares, 2)),
            dma((back,)),
            dma((back,)),
            dma((back + 1,)),
            dma((back + 1,)),
            dma((heads, blocks)),
            dma((heads, blocks)),
            dma((heads, blocks)),
            dma((heads, blocks)),
            dma((servers,)),
            dma((servers,)),
        ],
        compiler_params=pltpu.CompilerParams(
            collective_id=0, has_side_effects=True, vmem_limit_bytes=56 * 1024 * 1024
        ),
        cost_estimate=pl.CostEstimate(
            flops=4 * 10**9, bytes_accessed=8 * 2**20, transcendentals=2 * 10**6
        ),
    )(
        doc_lengths,
        task_server,
        hidden_in,
        norm_gain[None, :],
        freq,
        q_weight,
        kv_weight,
        o_weight,
    )
    return (layer_out, lse.reshape(1, servers, 1, BLOCK))


def solution(mesh):
    placed = (
        P(("group", "tok"), None),
        P(),
        P("tok", ("head", "sub")),
        P("tok", ("head", "sub")),
        P(("head", "sub"), "tok"),
        P("group"),
        P("group", None),
    )
    sizes = tuple(mesh.shape[name] for name in ("group", "tok", "head", "sub"))
    return jax.shard_map(
        functools.partial(body, sizes),
        mesh=mesh,
        in_specs=placed,
        out_specs=(
            P(("group", "tok"), ("head", "sub")),
            P(("group", "tok", "sub"), None, "head", None),
        ),
        check_vma=False,
    )
```

```python
import functools

import jax
import jax.numpy as jnp
from jax import lax
from jax.experimental import pallas as pl
from jax.experimental.pallas import tpu as pltpu
from jax.sharding import PartitionSpec as P

BLOCK = 128
HEAD = 128
DOCMAX = 1024
rope_base = 500000.0
norm_eps = 1e-05
masked_score = -1e30
MESH = pl.DeviceIdType.MESH


def kernel(
    sizes,
    doc_ref,
    table_ref,
    hid_ref,
    gain_ref,
    freq_ref,
    q_ref,
    kv_ref,
    o_ref,
    out_ref,
    lse_ref,
    hid,
    normed,
    qw,
    kvw,
    o_stage,
    wo,
    q_acc,
    kv_acc,
    cos_buf,
    sin_buf,
    queries,
    window,
    att,
    lse_mine,
    lse_all,
    loc_sem,
    z_send,
    z_recv,
    y_send,
    y_recv,
    o_send,
    o_recv,
    k_send,
    k_recv,
    kc_send,
    kc_recv,
    a_send,
    a_recv,
    ac_send,
    ac_recv,
    l_send,
    l_recv,
):
    groups, toks, heads, subs = sizes
    y = lax.axis_index("group")
    t = lax.axis_index("tok")
    x = lax.axis_index("head")
    c = lax.axis_index("sub")
    rows, width = hid.shape
    depth = q_ref.shape[0]
    half = depth // 2
    o_half = o_ref.shape[0] // 2
    shares = heads * subs
    mine = x * subs + c
    blocks = rows // BLOCK
    heads_here = q_ref.shape[1] // HEAD
    back = DOCMAX // rows
    docs = doc_ref.shape[0]
    tasks = blocks * heads_here
    sent = []

    def at_half(ref, index, size):
        return ref.at[pl.ds(pl.multiple_of(index * size, size), size)]

    def when(cond, fn):
        if cond is True:
            fn()
        else:
            pl.when(cond)(fn)

    def send(cond, src, dst, send_sem, recv_sem, device):
        copy = pltpu.make_async_remote_copy(
            src_ref=src,
            dst_ref=dst,
            send_sem=send_sem,
            recv_sem=recv_sem,
            device_id=device,
            device_id_type=MESH,
        )
        when(cond, copy.start)
        sent.append((cond, copy))

    def arrived(cond, dst, sem):
        when(cond, pltpu.make_async_copy(dst, dst, sem).wait)

    load_hid = pltpu.make_async_copy(hid_ref, hid, loc_sem.at[0])
    load_q = pltpu.make_async_copy(q_ref, qw.at[t], loc_sem.at[1])
    load_kv = pltpu.make_async_copy(kv_ref, kvw.at[t], loc_sem.at[2])
    load_hid.start()
    load_q.start()
    load_kv.start()

    barrier = pltpu.get_barrier_semaphore()
    count = 0
    for dy in range(groups):
        for dx in range(heads):
            for dc in range(subs):
                if dy or dx or dc:
                    pl.semaphore_signal(
                        barrier,
                        inc=1,
                        device_id=(
                            lax.rem(y + dy, groups),
                            t,
                            lax.rem(x + dx, heads),
                            lax.rem(c + dc, subs),
                        ),
                        device_id_type=MESH,
                    )
                    count += 1
    for dt in range(1, toks):
        for dc in range(subs):
            pl.semaphore_signal(
                barrier,
                inc=1,
                device_id=(y, lax.rem(t + dt, toks), x, lax.rem(c + dc, subs)),
                device_id_type=MESH,
            )
            count += 1
    pl.semaphore_wait(barrier, count)

    slots = (qw, kvw, o_stage)

    def piece(array, shard):
        if array == 2:
            return o_stage.at[shard]
        return at_half(slots[array].at[shard], y, half)

    def pass_on(array, shard, cond, src, direction):
        target = t + (1 if direction == 0 else -1)
        inside = (target < toks) if direction == 0 else (target >= 0)
        send(
            cond & inside,
            src,
            piece(array, shard),
            z_send.at[array, direction, shard],
            z_recv.at[array, shard],
            (y, target, x, c),
        )

    def spread_o(shard, cond, src):
        dest_x, dest_c = shard // subs, lax.rem(shard, subs)
        dst = wo.at[mine, pl.ds(pl.multiple_of(y * o_half, o_half), o_half)]
        for dy in range(groups):
            dest_y = lax.rem(y + dy, groups)
            remote = cond if dy else cond & (shard != mine)
            send(
                remote,
                src,
                dst,
                o_send.at[shard, dy],
                o_recv.at[mine, y],
                (dest_y, t, dest_x, dest_c),
            )
        when(
            cond & (shard == mine),
            pltpu.make_async_copy(src, dst, o_recv.at[mine, y]).start,
        )

    yes = t >= 0
    own = (at_half(q_ref, y, half), at_half(kv_ref, y, half), at_half(o_ref, y, o_half))
    for array in range(2):
        for direction in range(2):
            pass_on(array, t, yes, own[array], direction)
    spread_o(t, yes, own[2])

    load_hid.wait()
    step_rows = 64

    def norm_rows(step, carry):
        at = pl.ds(pl.multiple_of(step * step_rows, step_rows), step_rows)
        part = hid[at, :].astype(jnp.float32)
        scale = lax.rsqrt(jnp.mean(part * part, axis=-1, keepdims=True) + norm_eps)
        result = (part * scale * gain_ref[...].astype(jnp.float32)).astype(jnp.bfloat16)
        for shard in range(toks):
            for side in range(2):
                first = shard * depth + side * half
                normed[shard, side, at, :] = result[:, first : first + half]
        return carry

    lax.fori_loop(0, rows // step_rows, norm_rows, 0)

    def doc_start(pos):
        start = jnp.zeros_like(pos)
        total = doc_ref[0] * 0
        for doc in range(docs):
            start = jnp.where(total <= pos, total, start)
            total = total + doc_ref[doc]
        return start

    def angles(step, carry):
        at = pl.ds(pl.multiple_of(step * BLOCK, BLOCK), BLOCK)
        pos = t * rows + step * BLOCK + lax.broadcasted_iota(jnp.int32, (BLOCK, HEAD), 0)
        angle = (pos - doc_start(pos)).astype(jnp.float32) * freq_ref[...]
        cos_buf[at, :] = jnp.cos(angle)
        sign = jnp.where(lax.broadcasted_iota(jnp.int32, (BLOCK, HEAD), 1) < HEAD // 2, -1.0, 1.0)
        sin_buf[at, :] = jnp.sin(angle) * sign
        return carry


    def project(shard, side, first=False):
        at = pl.ds(pl.multiple_of(side * half, half), half)
        part = normed[shard, side]
        q_part = jnp.dot(part, qw[shard, at, :], preferred_element_type=jnp.float32)
        kv_part = jnp.dot(part, kvw[shard, at, :], preferred_element_type=jnp.float32)
        if first:
            q_acc[...] = q_part
            kv_acc[...] = kv_part
        else:
            q_acc[...] += q_part
            kv_acc[...] += kv_part

    other = lax.rem(y + 1, groups)

    def from_step(k, direction):
        shard = t - k if direction == 0 else t + k
        return shard, (shard >= 0) if direction == 0 else (shard < toks)

    def other_halves(k):
        for direction in range(2):
            shard, valid = from_step(k, direction)
            for array in range(2):
                arrived(
                    valid, at_half(slots[array].at[shard], other, half), y_recv.at[array, shard]
                )
            pl.when(valid)(functools.partial(project, shard, other))

    def chain_o(k):
        for direction in range(2):
            shard, valid = from_step(k, direction)
            arrived(valid, o_stage.at[shard], z_recv.at[2, shard])
            pass_on(2, shard, valid, o_stage.at[shard], direction)
            spread_o(shard, valid, o_stage.at[shard])

    for k in range(1, toks):
        for direction in range(2):
            shard, valid = from_step(k, direction)
            for array in range(2):
                arrived(valid, piece(array, shard), z_recv.at[array, shard])
                pass_on(array, shard, valid, piece(array, shard), direction)
                send(
                    valid,
                    piece(array, shard),
                    piece(array, shard),
                    y_send.at[array, shard],
                    y_recv.at[array, shard],
                    (other, t, x, c),
                )
        if k == 1:
            for direction in range(2):
                pass_on(2, t, yes, own[2], direction)
        else:
            chain_o(k - 1)
        if k == 1:
            lax.fori_loop(0, blocks, angles, 0)
            load_q.wait()
            load_kv.wait()
            project(t, 0, first=True)
            project(t, 1)
        else:
            other_halves(k - 1)
        for direction in range(2):
            shard, valid = from_step(k, direction)
            pl.when(valid)(functools.partial(project, shard, y))
    other_halves(toks - 1)

    def rotated(u):
        return u * cos_buf[...] + pltpu.roll(u, HEAD // 2, 1) * sin_buf[...]

    kv_raw = kv_acc[...]
    own_rows = pl.ds(back * rows, rows)
    window[c, own_rows, :] = jnp.where(c == 0, rotated(kv_raw), kv_raw).astype(jnp.bfloat16)
    twin = lax.rem(c + 1, subs)
    for j in range(1, back + 1):
        send(
            t + j < toks,
            window.at[c, own_rows],
            window.at[c, pl.ds((back - j) * rows, rows)],
            k_send.at[j - 1],
            k_recv.at[j - 1],
            (y, t + j, x, c),
        )
    send(
        True,
        window.at[c, own_rows],
        window.at[c, own_rows],
        kc_send.at[0],
        kc_recv.at[0],
        (y, t, x, twin),
    )
    for h in range(heads_here):
        turned = rotated(q_acc[:, h * HEAD : (h + 1) * HEAD]).astype(jnp.bfloat16)
        for b in range(blocks):
            queries[b, h * BLOCK : (h + 1) * BLOCK, :] = turned[b * BLOCK : (b + 1) * BLOCK]
    for j in range(1, back + 1):
        at = pl.ds((back - j) * rows, rows)

        def blank(at=at):
            window[:, at, :] = jnp.zeros((2, rows, HEAD), jnp.bfloat16)

        pl.when(t < j)(blank)
        arrived(t >= j, window.at[c, at], k_recv.at[j - 1])
        send(
            t >= j,
            window.at[c, at],
            window.at[c, at],
            kc_send.at[j],
            kc_recv.at[j],
            (y, t, x, twin),
        )
    chain_o(toks - 1)
    arrived(True, window.at[twin, own_rows], kc_recv.at[0])
    for j in range(1, back + 1):
        at = pl.ds((back - j) * rows, rows)
        arrived(t >= j, window.at[twin, at], kc_recv.at[j])

    reach = DOCMAX + BLOCK
    stack = heads_here * BLOCK
    scale = HEAD ** (-0.5)
    diagonal = lax.broadcasted_iota(jnp.int32, (BLOCK, BLOCK), 0) == lax.broadcasted_iota(
        jnp.int32, (BLOCK, BLOCK), 1
    )
    def forward(b):
        for dx in range(1, heads):
            source = lax.rem(x + dx, heads)
            arrived(True, att.at[source * subs + c, b], a_recv.at[source, b])
            send(
                True,
                att.at[source * subs + c, b],
                att.at[source * subs + c, b],
                ac_send.at[dx, b],
                ac_recv.at[source, b],
                (y, t, x, twin),
            )

    for b in range(blocks):
        keys = window[0, b * BLOCK : b * BLOCK + reach, :]
        values = window[1, b * BLOCK : b * BLOCK + reach, :]
        scores = (
            lax.dot_general(
                queries[b], keys, (((1,), (1,)), ((), ())), preferred_element_type=jnp.float32
            )
            * scale
        )
        row = lax.broadcasted_iota(jnp.int32, (stack, 1), 0)
        pos = t * rows + b * BLOCK + lax.rem(row, BLOCK)
        start = doc_start(pos)
        key_pos = (t - back) * rows + b * BLOCK + lax.broadcasted_iota(jnp.int32, (1, reach), 1)
        allowed = (key_pos >= start) & (key_pos <= pos)
        scores = jnp.where(allowed, scores, masked_score)
        peak = jnp.max(scores, axis=-1, keepdims=True)
        weights = jnp.exp(scores - peak)
        denom = jnp.sum(weights, axis=-1, keepdims=True)
        mixed = jnp.dot(weights.astype(jnp.bfloat16), values, preferred_element_type=jnp.float32)
        mixed = (mixed / denom).astype(jnp.bfloat16)
        spread = peak + jnp.log(denom)
        for h in range(heads_here):
            att[mine, b, :, h * HEAD : (h + 1) * HEAD] = mixed[h * BLOCK : (h + 1) * BLOCK]
            lse_mine[pl.ds(b * heads_here + h, 1), :] = jnp.sum(
                jnp.where(diagonal, spread[h * BLOCK : (h + 1) * BLOCK], 0.0),
                axis=0,
                keepdims=True,
            )
        for dx in range(1, heads):
            send(
                True,
                att.at[mine, b],
                att.at[mine, b],
                a_send.at[dx, b],
                a_recv.at[x, b],
                (y, t, lax.rem(x + dx, heads), c),
            )
        send(
            True,
            att.at[mine, b],
            att.at[mine, b],
            ac_send.at[0, b],
            ac_recv.at[x, b],
            (y, t, x, twin),
        )
        if b:
            forward(b - 1)

    me = t * subs + c
    for dt in range(toks):
        for dc in range(subs):
            if dt or dc:
                send(
                    True,
                    lse_mine,
                    lse_all.at[me],
                    l_send.at[dt * subs + dc],
                    l_recv.at[me],
                    (y, lax.rem(t + dt, toks), x, lax.rem(c + dc, subs)),
                )
    lse_all[me] = lse_mine[...]

    for r in range(shares):
        for side in range(2):
            dst = wo.at[r, pl.ds(side * o_half, o_half)]
            arrived(True, dst, o_recv.at[r, side])
    share_cols = out_ref.shape[1]
    columns = pl.ds(pl.multiple_of(mine * share_cols, share_cols), share_cols)
    pair = 2
    for first in range(0, blocks, pair):
        if first + pair == blocks:
            forward(blocks - 1)
        for b in range(first, first + pair):
            for dx in range(heads):
                source = lax.rem(x + dx, heads)
                arrived(True, att.at[source * subs + twin, b], ac_recv.at[source, b])
        at = slice(first * BLOCK, (first + pair) * BLOCK)
        summed = jnp.zeros((pair * BLOCK, share_cols), jnp.float32)
        for r in range(shares):
            product = jnp.dot(
                att[r, first : first + pair].reshape(pair * BLOCK, att.shape[3]),
                wo[r],
                preferred_element_type=jnp.float32,
            )
            summed += product.astype(jnp.bfloat16).astype(jnp.float32)
        out_ref[at, :] = (hid[at, columns].astype(jnp.float32) + summed).astype(jnp.bfloat16)

    group_heads = heads_here * subs
    for dt in range(toks):
        for dc in range(subs):
            source = lax.rem(t + dt, toks) * subs + lax.rem(c + dc, subs)
            if dt or dc:
                arrived(True, lse_all.at[source], l_recv.at[source])
    for source in range(toks * subs):
        kept = jnp.zeros((1, BLOCK), jnp.float32)
        for task in range(tasks):
            server = table_ref[
                (source // subs) * blocks + task // heads_here,
                x * group_heads + (source % subs) * heads_here + task % heads_here,
            ]
            kept = kept + jnp.where(server == me, lse_all[source, task : task + 1, :], 0.0)
        lse_ref[source : source + 1, :] = kept

    for cond, copy in sent:
        when(cond, copy.wait_send)


def body(sizes, hidden_in, norm_gain, q_weight, kv_weight, o_weight, doc_lengths, task_server):
    groups, toks, heads, subs = sizes
    rows, width = hidden_in.shape
    depth, q_cols = q_weight.shape
    o_rows, o_cols = o_weight.shape
    shares = heads * subs
    assert groups == 2 and subs == 2 and toks == shares
    assert width // shares == o_cols and DOCMAX % rows == 0
    blocks = rows // BLOCK
    heads_here = q_cols // HEAD
    back = DOCMAX // rows
    tasks = blocks * heads_here
    servers = toks * subs
    half = jnp.arange(HEAD // 2, dtype=jnp.float32)
    freq = rope_base ** (-(half * 2.0 / HEAD))
    freq = jnp.concatenate([freq, freq])[None, :]
    bf16, f32 = jnp.bfloat16, jnp.float32
    dma = pltpu.SemaphoreType.DMA
    any_spec = pl.BlockSpec(memory_space=pl.ANY)
    vmem = pl.BlockSpec(memory_space=pltpu.VMEM)
    smem = pl.BlockSpec(memory_space=pltpu.SMEM)
    layer_out, lse = pl.pallas_call(
        functools.partial(kernel, sizes),
        out_shape=(
            jax.ShapeDtypeStruct((rows, o_cols), bf16),
            jax.ShapeDtypeStruct((servers, BLOCK), f32),
        ),
        in_specs=[smem, smem, any_spec, vmem, vmem, any_spec, any_spec, any_spec],
        out_specs=(vmem, vmem),
        scratch_shapes=[
            pltpu.VMEM((rows, width), bf16),
            pltpu.VMEM((toks, 2, rows, depth // 2), bf16),
            pltpu.VMEM((toks, depth, q_cols), bf16),
            pltpu.VMEM((toks, depth, HEAD), bf16),
            pltpu.VMEM((toks, o_rows // 2, o_cols), bf16),
            pltpu.VMEM((shares, o_rows, o_cols), bf16),
            pltpu.VMEM((rows, q_cols), f32),
            pltpu.VMEM((rows, HEAD), f32),
            pltpu.VMEM((rows, HEAD), f32),
            pltpu.VMEM((rows, HEAD), f32),
            pltpu.VMEM((blocks, heads_here * BLOCK, HEAD), bf16),
            pltpu.VMEM((2, (back + 1) * rows, HEAD), bf16),
            pltpu.VMEM((shares, blocks, BLOCK, q_cols), bf16),
            pltpu.VMEM((tasks, BLOCK), f32),
            pltpu.VMEM((servers, tasks, BLOCK), f32),
            dma((3,)),
            dma((3, 2, toks)),
            dma((3, toks)),
            dma((2, toks)),
            dma((2, toks)),
            dma((toks, groups)),
            dma((shares, 2)),
            dma((back,)),
            dma((back,)),
            dma((back + 1,)),
            dma((back + 1,)),
            dma((heads, blocks)),
            dma((heads, blocks)),
            dma((heads, blocks)),
            dma((heads, blocks)),
            dma((servers,)),
            dma((servers,)),
        ],
        compiler_params=pltpu.CompilerParams(
            collective_id=0, has_side_effects=True, vmem_limit_bytes=56 * 1024 * 1024
        ),
        cost_estimate=pl.CostEstimate(
            flops=4 * 10**9, bytes_accessed=8 * 2**20, transcendentals=2 * 10**6
        ),
    )(
        doc_lengths,
        task_server,
        hidden_in,
        norm_gain[None, :],
        freq,
        q_weight,
        kv_weight,
        o_weight,
    )
    return (layer_out, lse.reshape(1, servers, 1, BLOCK))


def solution(mesh):
    placed = (
        P(("group", "tok"), None),
        P(),
        P("tok", ("head", "sub")),
        P("tok", ("head", "sub")),
        P(("head", "sub"), "tok"),
        P("group"),
        P("group", None),
    )
    sizes = tuple(mesh.shape[name] for name in ("group", "tok", "head", "sub"))
    return jax.shard_map(
        functools.partial(body, sizes),
        mesh=mesh,
        in_specs=placed,
        out_specs=(
            P(("group", "tok"), ("head", "sub")),
            P(("group", "tok", "sub"), None, "head", None),
        ),
        check_vma=False,
    )
```

```python
import functools

import jax
import jax.numpy as jnp
from jax import lax
from jax.experimental import pallas as pl
from jax.experimental.pallas import tpu as pltpu
from jax.sharding import PartitionSpec as P

BLOCK = 128
HEAD = 128
DOCMAX = 1024
rope_base = 500000.0
norm_eps = 1e-05
masked_score = -1e30
MESH = pl.DeviceIdType.MESH


def kernel(
    sizes,
    doc_ref,
    table_ref,
    hid_ref,
    gain_ref,
    freq_ref,
    q_ref,
    kv_ref,
    o_ref,
    out_ref,
    lse_ref,
    hid,
    normed,
    qw,
    kvw,
    o_stage,
    wo,
    q_acc,
    kv_acc,
    cos_buf,
    sin_buf,
    queries,
    window,
    att,
    lse_mine,
    lse_all,
    loc_sem,
    z_send,
    z_recv,
    y_send,
    y_recv,
    o_send,
    o_recv,
    k_send,
    k_recv,
    kc_send,
    kc_recv,
    a_send,
    a_recv,
    ac_send,
    ac_recv,
    l_send,
    l_recv,
):
    groups, toks, heads, subs = sizes
    y = lax.axis_index("group")
    t = lax.axis_index("tok")
    x = lax.axis_index("head")
    c = lax.axis_index("sub")
    rows, width = hid.shape
    depth = q_ref.shape[0]
    half = depth // 2
    o_half = o_ref.shape[0] // 2
    shares = heads * subs
    mine = x * subs + c
    blocks = rows // BLOCK
    heads_here = q_ref.shape[1] // HEAD
    back = DOCMAX // rows
    docs = doc_ref.shape[0]
    tasks = blocks * heads_here
    sent = []

    def at_half(ref, index, size):
        return ref.at[pl.ds(pl.multiple_of(index * size, size), size)]

    def when(cond, fn):
        if cond is True:
            fn()
        else:
            pl.when(cond)(fn)

    def send(cond, src, dst, send_sem, recv_sem, device):
        copy = pltpu.make_async_remote_copy(
            src_ref=src,
            dst_ref=dst,
            send_sem=send_sem,
            recv_sem=recv_sem,
            device_id=device,
            device_id_type=MESH,
        )
        when(cond, copy.start)
        sent.append((cond, copy))

    def arrived(cond, dst, sem):
        when(cond, pltpu.make_async_copy(dst, dst, sem).wait)

    load_hid = pltpu.make_async_copy(hid_ref, hid, loc_sem.at[0])
    load_q = pltpu.make_async_copy(q_ref, qw.at[t], loc_sem.at[1])
    load_kv = pltpu.make_async_copy(kv_ref, kvw.at[t], loc_sem.at[2])
    load_hid.start()
    load_q.start()
    load_kv.start()

    barrier = pltpu.get_barrier_semaphore()
    count = 0
    for dy in range(groups):
        for dx in range(heads):
            for dc in range(subs):
                if dy or dx or dc:
                    pl.semaphore_signal(
                        barrier,
                        inc=1,
                        device_id=(
                            lax.rem(y + dy, groups),
                            t,
                            lax.rem(x + dx, heads),
                            lax.rem(c + dc, subs),
                        ),
                        device_id_type=MESH,
                    )
                    count += 1
    for dt in range(1, toks):
        for dc in range(subs):
            pl.semaphore_signal(
                barrier,
                inc=1,
                device_id=(y, lax.rem(t + dt, toks), x, lax.rem(c + dc, subs)),
                device_id_type=MESH,
            )
            count += 1
    pl.semaphore_wait(barrier, count)

    slots = (qw, kvw, o_stage)

    def piece(array, shard):
        if array == 2:
            return o_stage.at[shard]
        return at_half(slots[array].at[shard], y, half)

    def pass_on(array, shard, cond, src, direction):
        target = t + (1 if direction == 0 else -1)
        inside = (target < toks) if direction == 0 else (target >= 0)
        send(
            cond & inside,
            src,
            piece(array, shard),
            z_send.at[array, direction, shard],
            z_recv.at[array, shard],
            (y, target, x, c),
        )

    def spread_o(shard, cond, src):
        dest_x, dest_c = shard // subs, lax.rem(shard, subs)
        dst = wo.at[mine, pl.ds(pl.multiple_of(y * o_half, o_half), o_half)]
        for dy in range(groups):
            dest_y = lax.rem(y + dy, groups)
            remote = cond if dy else cond & (shard != mine)
            send(
                remote,
                src,
                dst,
                o_send.at[shard, dy],
                o_recv.at[mine, y],
                (dest_y, t, dest_x, dest_c),
            )
        when(
            cond & (shard == mine),
            pltpu.make_async_copy(src, dst, o_recv.at[mine, y]).start,
        )

    yes = t >= 0
    own = (at_half(q_ref, y, half), at_half(kv_ref, y, half), at_half(o_ref, y, o_half))
    for array in range(2):
        for direction in range(2):
            pass_on(array, t, yes, own[array], direction)
    spread_o(t, yes, own[2])

    load_hid.wait()
    step_rows = 64

    def norm_rows(step, carry):
        at = pl.ds(pl.multiple_of(step * step_rows, step_rows), step_rows)
        part = hid[at, :].astype(jnp.float32)
        scale = lax.rsqrt(jnp.mean(part * part, axis=-1, keepdims=True) + norm_eps)
        result = (part * scale * gain_ref[...].astype(jnp.float32)).astype(jnp.bfloat16)
        for shard in range(toks):
            for side in range(2):
                first = shard * depth + side * half
                normed[shard, side, at, :] = result[:, first : first + half]
        return carry

    lax.fori_loop(0, rows // step_rows, norm_rows, 0)

    def doc_start(pos):
        start = jnp.zeros_like(pos)
        total = doc_ref[0] * 0
        for doc in range(docs):
            start = jnp.where(total <= pos, total, start)
            total = total + doc_ref[doc]
        return start

    def angles(step, carry):
        at = pl.ds(pl.multiple_of(step * BLOCK, BLOCK), BLOCK)
        pos = t * rows + step * BLOCK + lax.broadcasted_iota(jnp.int32, (BLOCK, HEAD), 0)
        angle = (pos - doc_start(pos)).astype(jnp.float32) * freq_ref[...]
        cos_buf[at, :] = jnp.cos(angle)
        sign = jnp.where(lax.broadcasted_iota(jnp.int32, (BLOCK, HEAD), 1) < HEAD // 2, -1.0, 1.0)
        sin_buf[at, :] = jnp.sin(angle) * sign
        return carry


    def project(shard, side, first=False):
        at = pl.ds(pl.multiple_of(side * half, half), half)
        part = normed[shard, side]
        q_part = jnp.dot(part, qw[shard, at, :], preferred_element_type=jnp.float32)
        kv_part = jnp.dot(part, kvw[shard, at, :], preferred_element_type=jnp.float32)
        if first:
            q_acc[...] = q_part
            kv_acc[...] = kv_part
        else:
            q_acc[...] += q_part
            kv_acc[...] += kv_part

    other = lax.rem(y + 1, groups)

    def from_step(k, direction):
        shard = t - k if direction == 0 else t + k
        return shard, (shard >= 0) if direction == 0 else (shard < toks)

    def other_halves(k):
        for direction in range(2):
            shard, valid = from_step(k, direction)
            for array in range(2):
                arrived(
                    valid, at_half(slots[array].at[shard], other, half), y_recv.at[array, shard]
                )
            pl.when(valid)(functools.partial(project, shard, other))

    def chain_o(k):
        for direction in range(2):
            shard, valid = from_step(k, direction)
            arrived(valid, o_stage.at[shard], z_recv.at[2, shard])
            spread_o(shard, valid, o_stage.at[shard])

    for k in range(1, toks):
        for direction in range(2):
            shard, valid = from_step(k, direction)
            for array in range(2):
                arrived(valid, piece(array, shard), z_recv.at[array, shard])
                pass_on(array, shard, valid, piece(array, shard), direction)
                send(
                    valid,
                    piece(array, shard),
                    piece(array, shard),
                    y_send.at[array, shard],
                    y_recv.at[array, shard],
                    (other, t, x, c),
                )
        if k == 1:
            for j in range(1, toks):
                for target in (t - j, t + j):
                    send(
                        (target >= 0) & (target < toks),
                        own[2],
                        o_stage.at[t],
                        z_send.at[2, 0, target],
                        z_recv.at[2, t],
                        (y, target, x, c),
                    )
        if k == 1:
            lax.fori_loop(0, blocks, angles, 0)
            load_q.wait()
            load_kv.wait()
            project(t, 0, first=True)
            project(t, 1)
        else:
            other_halves(k - 1)
        for direction in range(2):
            shard, valid = from_step(k, direction)
            pl.when(valid)(functools.partial(project, shard, y))
    chain_o(1)
    other_halves(toks - 1)

    def rotated(u):
        return u * cos_buf[...] + pltpu.roll(u, HEAD // 2, 1) * sin_buf[...]

    kv_raw = kv_acc[...]
    own_rows = pl.ds(back * rows, rows)
    window[c, own_rows, :] = jnp.where(c == 0, rotated(kv_raw), kv_raw).astype(jnp.bfloat16)
    twin = lax.rem(c + 1, subs)
    for j in range(1, back + 1):
        send(
            t + j < toks,
            window.at[c, own_rows],
            window.at[c, pl.ds((back - j) * rows, rows)],
            k_send.at[j - 1],
            k_recv.at[j - 1],
            (y, t + j, x, c),
        )
    send(
        True,
        window.at[c, own_rows],
        window.at[c, own_rows],
        kc_send.at[0],
        kc_recv.at[0],
        (y, t, x, twin),
    )
    for h in range(heads_here):
        turned = rotated(q_acc[:, h * HEAD : (h + 1) * HEAD]).astype(jnp.bfloat16)
        for b in range(blocks):
            queries[b, h * BLOCK : (h + 1) * BLOCK, :] = turned[b * BLOCK : (b + 1) * BLOCK]
    for j in range(1, back + 1):
        at = pl.ds((back - j) * rows, rows)

        def blank(at=at):
            window[:, at, :] = jnp.zeros((2, rows, HEAD), jnp.bfloat16)

        pl.when(t < j)(blank)
        arrived(t >= j, window.at[c, at], k_recv.at[j - 1])
        send(
            t >= j,
            window.at[c, at],
            window.at[c, at],
            kc_send.at[j],
            kc_recv.at[j],
            (y, t, x, twin),
        )
    for k in range(2, toks):
        chain_o(k)
    arrived(True, window.at[twin, own_rows], kc_recv.at[0])
    for j in range(1, back + 1):
        at = pl.ds((back - j) * rows, rows)
        arrived(t >= j, window.at[twin, at], kc_recv.at[j])

    reach = DOCMAX + BLOCK
    stack = heads_here * BLOCK
    scale = HEAD ** (-0.5)
    diagonal = lax.broadcasted_iota(jnp.int32, (BLOCK, BLOCK), 0) == lax.broadcasted_iota(
        jnp.int32, (BLOCK, BLOCK), 1
    )
    def forward(b):
        for dx in range(1, heads):
            source = lax.rem(x + dx, heads)
            arrived(True, att.at[source * subs + c, b], a_recv.at[source, b])
            send(
                True,
                att.at[source * subs + c, b],
                att.at[source * subs + c, b],
                ac_send.at[dx, b],
                ac_recv.at[source, b],
                (y, t, x, twin),
            )

    for b in range(blocks):
        keys = window[0, b * BLOCK : b * BLOCK + reach, :]
        values = window[1, b * BLOCK : b * BLOCK + reach, :]
        scores = (
            lax.dot_general(
                queries[b], keys, (((1,), (1,)), ((), ())), preferred_element_type=jnp.float32
            )
            * scale
        )
        row = lax.broadcasted_iota(jnp.int32, (stack, 1), 0)
        pos = t * rows + b * BLOCK + lax.rem(row, BLOCK)
        start = doc_start(pos)
        key_pos = (t - back) * rows + b * BLOCK + lax.broadcasted_iota(jnp.int32, (1, reach), 1)
        allowed = (key_pos >= start) & (key_pos <= pos)
        scores = jnp.where(allowed, scores, masked_score)
        peak = jnp.max(scores, axis=-1, keepdims=True)
        weights = jnp.exp(scores - peak)
        denom = jnp.sum(weights, axis=-1, keepdims=True)
        mixed = jnp.dot(weights.astype(jnp.bfloat16), values, preferred_element_type=jnp.float32)
        mixed = (mixed / denom).astype(jnp.bfloat16)
        spread = peak + jnp.log(denom)
        for h in range(heads_here):
            att[mine, b, :, h * HEAD : (h + 1) * HEAD] = mixed[h * BLOCK : (h + 1) * BLOCK]
            lse_mine[pl.ds(b * heads_here + h, 1), :] = jnp.sum(
                jnp.where(diagonal, spread[h * BLOCK : (h + 1) * BLOCK], 0.0),
                axis=0,
                keepdims=True,
            )
        for dx in range(1, heads):
            send(
                True,
                att.at[mine, b],
                att.at[mine, b],
                a_send.at[dx, b],
                a_recv.at[x, b],
                (y, t, lax.rem(x + dx, heads), c),
            )
        send(
            True,
            att.at[mine, b],
            att.at[mine, b],
            ac_send.at[0, b],
            ac_recv.at[x, b],
            (y, t, x, twin),
        )
        if b:
            forward(b - 1)

    me = t * subs + c
    for dt in range(toks):
        for dc in range(subs):
            if dt or dc:
                send(
                    True,
                    lse_mine,
                    lse_all.at[me],
                    l_send.at[dt * subs + dc],
                    l_recv.at[me],
                    (y, lax.rem(t + dt, toks), x, lax.rem(c + dc, subs)),
                )
    lse_all[me] = lse_mine[...]

    for r in range(shares):
        for side in range(2):
            dst = wo.at[r, pl.ds(side * o_half, o_half)]
            arrived(True, dst, o_recv.at[r, side])
    share_cols = out_ref.shape[1]
    columns = pl.ds(pl.multiple_of(mine * share_cols, share_cols), share_cols)
    pair = 2
    for first in range(0, blocks, pair):
        if first + pair == blocks:
            forward(blocks - 1)
        for b in range(first, first + pair):
            for dx in range(heads):
                source = lax.rem(x + dx, heads)
                arrived(True, att.at[source * subs + twin, b], ac_recv.at[source, b])
        at = slice(first * BLOCK, (first + pair) * BLOCK)
        summed = jnp.zeros((pair * BLOCK, share_cols), jnp.float32)
        for r in range(shares):
            product = jnp.dot(
                att[r, first : first + pair].reshape(pair * BLOCK, att.shape[3]),
                wo[r],
                preferred_element_type=jnp.float32,
            )
            summed += product.astype(jnp.bfloat16).astype(jnp.float32)
        out_ref[at, :] = (hid[at, columns].astype(jnp.float32) + summed).astype(jnp.bfloat16)

    group_heads = heads_here * subs
    for dt in range(toks):
        for dc in range(subs):
            source = lax.rem(t + dt, toks) * subs + lax.rem(c + dc, subs)
            if dt or dc:
                arrived(True, lse_all.at[source], l_recv.at[source])
    for source in range(toks * subs):
        kept = jnp.zeros((1, BLOCK), jnp.float32)
        for task in range(tasks):
            server = table_ref[
                (source // subs) * blocks + task // heads_here,
                x * group_heads + (source % subs) * heads_here + task % heads_here,
            ]
            kept = kept + jnp.where(server == me, lse_all[source, task : task + 1, :], 0.0)
        lse_ref[source : source + 1, :] = kept

    for cond, copy in sent:
        when(cond, copy.wait_send)


def body(sizes, hidden_in, norm_gain, q_weight, kv_weight, o_weight, doc_lengths, task_server):
    groups, toks, heads, subs = sizes
    rows, width = hidden_in.shape
    depth, q_cols = q_weight.shape
    o_rows, o_cols = o_weight.shape
    shares = heads * subs
    assert groups == 2 and subs == 2 and toks == shares
    assert width // shares == o_cols and DOCMAX % rows == 0
    blocks = rows // BLOCK
    heads_here = q_cols // HEAD
    back = DOCMAX // rows
    tasks = blocks * heads_here
    servers = toks * subs
    half = jnp.arange(HEAD // 2, dtype=jnp.float32)
    freq = rope_base ** (-(half * 2.0 / HEAD))
    freq = jnp.concatenate([freq, freq])[None, :]
    bf16, f32 = jnp.bfloat16, jnp.float32
    dma = pltpu.SemaphoreType.DMA
    any_spec = pl.BlockSpec(memory_space=pl.ANY)
    vmem = pl.BlockSpec(memory_space=pltpu.VMEM)
    smem = pl.BlockSpec(memory_space=pltpu.SMEM)
    layer_out, lse = pl.pallas_call(
        functools.partial(kernel, sizes),
        out_shape=(
            jax.ShapeDtypeStruct((rows, o_cols), bf16),
            jax.ShapeDtypeStruct((servers, BLOCK), f32),
        ),
        in_specs=[smem, smem, any_spec, vmem, vmem, any_spec, any_spec, any_spec],
        out_specs=(vmem, vmem),
        scratch_shapes=[
            pltpu.VMEM((rows, width), bf16),
            pltpu.VMEM((toks, 2, rows, depth // 2), bf16),
            pltpu.VMEM((toks, depth, q_cols), bf16),
            pltpu.VMEM((toks, depth, HEAD), bf16),
            pltpu.VMEM((toks, o_rows // 2, o_cols), bf16),
            pltpu.VMEM((shares, o_rows, o_cols), bf16),
            pltpu.VMEM((rows, q_cols), f32),
            pltpu.VMEM((rows, HEAD), f32),
            pltpu.VMEM((rows, HEAD), f32),
            pltpu.VMEM((rows, HEAD), f32),
            pltpu.VMEM((blocks, heads_here * BLOCK, HEAD), bf16),
            pltpu.VMEM((2, (back + 1) * rows, HEAD), bf16),
            pltpu.VMEM((shares, blocks, BLOCK, q_cols), bf16),
            pltpu.VMEM((tasks, BLOCK), f32),
            pltpu.VMEM((servers, tasks, BLOCK), f32),
            dma((3,)),
            dma((3, 2, toks)),
            dma((3, toks)),
            dma((2, toks)),
            dma((2, toks)),
            dma((toks, groups)),
            dma((shares, 2)),
            dma((back,)),
            dma((back,)),
            dma((back + 1,)),
            dma((back + 1,)),
            dma((heads, blocks)),
            dma((heads, blocks)),
            dma((heads, blocks)),
            dma((heads, blocks)),
            dma((servers,)),
            dma((servers,)),
        ],
        compiler_params=pltpu.CompilerParams(
            collective_id=0, has_side_effects=True, vmem_limit_bytes=56 * 1024 * 1024
        ),
        cost_estimate=pl.CostEstimate(
            flops=4 * 10**9, bytes_accessed=8 * 2**20, transcendentals=2 * 10**6
        ),
    )(
        doc_lengths,
        task_server,
        hidden_in,
        norm_gain[None, :],
        freq,
        q_weight,
        kv_weight,
        o_weight,
    )
    return (layer_out, lse.reshape(1, servers, 1, BLOCK))


def solution(mesh):
    placed = (
        P(("group", "tok"), None),
        P(),
        P("tok", ("head", "sub")),
        P("tok", ("head", "sub")),
        P(("head", "sub"), "tok"),
        P("group"),
        P("group", None),
    )
    sizes = tuple(mesh.shape[name] for name in ("group", "tok", "head", "sub"))
    return jax.shard_map(
        functools.partial(body, sizes),
        mesh=mesh,
        in_specs=placed,
        out_specs=(
            P(("group", "tok"), ("head", "sub")),
            P(("group", "tok", "sub"), None, "head", None),
        ),
        check_vma=False,
    )
```

```python
import functools

import jax
import jax.numpy as jnp
from jax import lax
from jax.experimental import pallas as pl
from jax.experimental.pallas import tpu as pltpu
from jax.sharding import PartitionSpec as P

BLOCK = 128
HEAD = 128
DOCMAX = 1024
rope_base = 500000.0
norm_eps = 1e-05
masked_score = -1e30
MESH = pl.DeviceIdType.MESH


def kernel(
    sizes,
    doc_ref,
    table_ref,
    hid_ref,
    gain_ref,
    freq_ref,
    q_ref,
    kv_ref,
    o_ref,
    out_ref,
    lse_ref,
    hid,
    normed,
    qw,
    kvw,
    o_stage,
    wo,
    q_acc,
    kv_acc,
    cos_buf,
    sin_buf,
    queries,
    window,
    att,
    lse_mine,
    lse_all,
    loc_sem,
    z_send,
    z_recv,
    y_send,
    y_recv,
    o_send,
    o_recv,
    k_send,
    k_recv,
    kc_send,
    kc_recv,
    a_send,
    a_recv,
    ac_send,
    ac_recv,
    l_send,
    l_recv,
):
    groups, toks, heads, subs = sizes
    y = lax.axis_index("group")
    t = lax.axis_index("tok")
    x = lax.axis_index("head")
    c = lax.axis_index("sub")
    rows, width = hid.shape
    depth = q_ref.shape[0]
    half = depth // 2
    o_half = o_ref.shape[0] // 2
    shares = heads * subs
    mine = x * subs + c
    blocks = rows // BLOCK
    heads_here = q_ref.shape[1] // HEAD
    back = DOCMAX // rows
    docs = doc_ref.shape[0]
    tasks = blocks * heads_here
    sent = []

    def at_half(ref, index, size):
        return ref.at[pl.ds(pl.multiple_of(index * size, size), size)]

    def when(cond, fn):
        if cond is True:
            fn()
        else:
            pl.when(cond)(fn)

    def send(cond, src, dst, send_sem, recv_sem, device):
        copy = pltpu.make_async_remote_copy(
            src_ref=src,
            dst_ref=dst,
            send_sem=send_sem,
            recv_sem=recv_sem,
            device_id=device,
            device_id_type=MESH,
        )
        when(cond, copy.start)
        sent.append((cond, copy))

    def arrived(cond, dst, sem):
        when(cond, pltpu.make_async_copy(dst, dst, sem).wait)

    load_hid = pltpu.make_async_copy(hid_ref, hid, loc_sem.at[0])
    load_q = pltpu.make_async_copy(q_ref, qw.at[t], loc_sem.at[1])
    load_kv = pltpu.make_async_copy(kv_ref, kvw.at[t], loc_sem.at[2])
    load_hid.start()
    load_q.start()
    load_kv.start()

    barrier = pltpu.get_barrier_semaphore()
    count = 0
    for dy in range(groups):
        for dx in range(heads):
            for dc in range(subs):
                if dy or dx or dc:
                    pl.semaphore_signal(
                        barrier,
                        inc=1,
                        device_id=(
                            lax.rem(y + dy, groups),
                            t,
                            lax.rem(x + dx, heads),
                            lax.rem(c + dc, subs),
                        ),
                        device_id_type=MESH,
                    )
                    count += 1
    for dt in range(1, toks):
        for dc in range(subs):
            pl.semaphore_signal(
                barrier,
                inc=1,
                device_id=(y, lax.rem(t + dt, toks), x, lax.rem(c + dc, subs)),
                device_id_type=MESH,
            )
            count += 1
    pl.semaphore_wait(barrier, count)

    slots = (qw, kvw, o_stage)

    def piece(array, shard):
        if array == 2:
            return o_stage.at[shard]
        return at_half(slots[array].at[shard], y, half)

    def pass_on(array, shard, cond, src, direction):
        target = t + (1 if direction == 0 else -1)
        inside = (target < toks) if direction == 0 else (target >= 0)
        send(
            cond & inside,
            src,
            piece(array, shard),
            z_send.at[array, direction, shard],
            z_recv.at[array, shard],
            (y, target, x, c),
        )

    def spread_o(shard, cond, src):
        dest_x, dest_c = shard // subs, lax.rem(shard, subs)
        dst = wo.at[mine, pl.ds(pl.multiple_of(y * o_half, o_half), o_half)]
        for dy in range(groups):
            dest_y = lax.rem(y + dy, groups)
            remote = cond if dy else cond & (shard != mine)
            send(
                remote,
                src,
                dst,
                o_send.at[shard, dy],
                o_recv.at[mine, y],
                (dest_y, t, dest_x, dest_c),
            )
        when(
            cond & (shard == mine),
            pltpu.make_async_copy(src, dst, o_recv.at[mine, y]).start,
        )

    yes = t >= 0
    own = (at_half(q_ref, y, half), at_half(kv_ref, y, half), at_half(o_ref, y, o_half))
    for array in range(2):
        for direction in range(2):
            pass_on(array, t, yes, own[array], direction)
    for direction in range(2):
        pass_on(2, t, yes, own[2], direction)
    spread_o(t, yes, own[2])

    load_hid.wait()
    step_rows = 64

    def norm_rows(step, carry):
        at = pl.ds(pl.multiple_of(step * step_rows, step_rows), step_rows)
        part = hid[at, :].astype(jnp.float32)
        scale = lax.rsqrt(jnp.mean(part * part, axis=-1, keepdims=True) + norm_eps)
        result = (part * scale * gain_ref[...].astype(jnp.float32)).astype(jnp.bfloat16)
        for shard in range(toks):
            for side in range(2):
                first = shard * depth + side * half
                normed[shard, side, at, :] = result[:, first : first + half]
        return carry

    lax.fori_loop(0, rows // step_rows, norm_rows, 0)

    def doc_start(pos):
        start = jnp.zeros_like(pos)
        total = doc_ref[0] * 0
        for doc in range(docs):
            start = jnp.where(total <= pos, total, start)
            total = total + doc_ref[doc]
        return start

    def angles(step, carry):
        at = pl.ds(pl.multiple_of(step * BLOCK, BLOCK), BLOCK)
        pos = t * rows + step * BLOCK + lax.broadcasted_iota(jnp.int32, (BLOCK, HEAD), 0)
        angle = (pos - doc_start(pos)).astype(jnp.float32) * freq_ref[...]
        cos_buf[at, :] = jnp.cos(angle)
        sign = jnp.where(lax.broadcasted_iota(jnp.int32, (BLOCK, HEAD), 1) < HEAD // 2, -1.0, 1.0)
        sin_buf[at, :] = jnp.sin(angle) * sign
        return carry

    lax.fori_loop(0, blocks, angles, 0)

    def project(shard, side, first=False):
        at = pl.ds(pl.multiple_of(side * half, half), half)
        part = normed[shard, side]
        q_part = jnp.dot(part, qw[shard, at, :], preferred_element_type=jnp.float32)
        kv_part = jnp.dot(part, kvw[shard, at, :], preferred_element_type=jnp.float32)
        if first:
            q_acc[...] = q_part
            kv_acc[...] = kv_part
        else:
            q_acc[...] += q_part
            kv_acc[...] += kv_part

    load_q.wait()
    load_kv.wait()
    project(t, 0, first=True)
    project(t, 1)

    other = lax.rem(y + 1, groups)
    for k in range(1, toks):
        for direction in range(2):
            shard = t - k if direction == 0 else t + k
            valid = (shard >= 0) if direction == 0 else (shard < toks)
            for array in range(2):
                arrived(valid, piece(array, shard), z_recv.at[array, shard])
                pass_on(array, shard, valid, piece(array, shard), direction)
                send(
                    valid,
                    piece(array, shard),
                    piece(array, shard),
                    y_send.at[array, shard],
                    y_recv.at[array, shard],
                    (other, t, x, c),
                )
        for direction in range(2):
            shard = t - k if direction == 0 else t + k
            valid = (shard >= 0) if direction == 0 else (shard < toks)
            pl.when(valid)(functools.partial(project, shard, y))
    for k in range(1, toks):
        for direction in range(2):
            shard = t - k if direction == 0 else t + k
            valid = (shard >= 0) if direction == 0 else (shard < toks)
            arrived(valid, o_stage.at[shard], z_recv.at[2, shard])
            pass_on(2, shard, valid, o_stage.at[shard], direction)
            spread_o(shard, valid, o_stage.at[shard])
            for array in range(2):
                arrived(
                    valid, at_half(slots[array].at[shard], other, half), y_recv.at[array, shard]
                )
            pl.when(valid)(functools.partial(project, shard, other))

    def rotated(u):
        return u * cos_buf[...] + pltpu.roll(u, HEAD // 2, 1) * sin_buf[...]

    kv_raw = kv_acc[...]
    own_rows = pl.ds(back * rows, rows)
    window[c, own_rows, :] = jnp.where(c == 0, rotated(kv_raw), kv_raw).astype(jnp.bfloat16)
    twin = lax.rem(c + 1, subs)
    for j in range(1, back + 1):
        send(
            t + j < toks,
            window.at[c, own_rows],
            window.at[c, pl.ds((back - j) * rows, rows)],
            k_send.at[j - 1],
            k_recv.at[j - 1],
            (y, t + j, x, c),
        )
    send(
        True,
        window.at[c, own_rows],
        window.at[c, own_rows],
        kc_send.at[0],
        kc_recv.at[0],
        (y, t, x, twin),
    )
    for h in range(heads_here):
        turned = rotated(q_acc[:, h * HEAD : (h + 1) * HEAD]).astype(jnp.bfloat16)
        for b in range(blocks):
            queries[b, h * BLOCK : (h + 1) * BLOCK, :] = turned[b * BLOCK : (b + 1) * BLOCK]
    for j in range(1, back + 1):
        at = pl.ds((back - j) * rows, rows)

        def blank(at=at):
            window[:, at, :] = jnp.zeros((2, rows, HEAD), jnp.bfloat16)

        pl.when(t < j)(blank)
        arrived(t >= j, window.at[c, at], k_recv.at[j - 1])
        send(
            t >= j,
            window.at[c, at],
            window.at[c, at],
            kc_send.at[j],
            kc_recv.at[j],
            (y, t, x, twin),
        )
    arrived(True, window.at[twin, own_rows], kc_recv.at[0])
    for j in range(1, back + 1):
        at = pl.ds((back - j) * rows, rows)
        arrived(t >= j, window.at[twin, at], kc_recv.at[j])

    reach = DOCMAX + BLOCK
    stack = heads_here * BLOCK
    scale = HEAD ** (-0.5)
    diagonal = lax.broadcasted_iota(jnp.int32, (BLOCK, BLOCK), 0) == lax.broadcasted_iota(
        jnp.int32, (BLOCK, BLOCK), 1
    )
    def forward(b):
        for dx in range(1, heads):
            source = lax.rem(x + dx, heads)
            arrived(True, att.at[source * subs + c, b], a_recv.at[source, b])
            send(
                True,
                att.at[source * subs + c, b],
                att.at[source * subs + c, b],
                ac_send.at[dx, b],
                ac_recv.at[source, b],
                (y, t, x, twin),
            )

    for b in range(blocks):
        keys = window[0, b * BLOCK : b * BLOCK + reach, :]
        values = window[1, b * BLOCK : b * BLOCK + reach, :]
        scores = (
            lax.dot_general(
                queries[b], keys, (((1,), (1,)), ((), ())), preferred_element_type=jnp.float32
            )
            * scale
        )
        row = lax.broadcasted_iota(jnp.int32, (stack, 1), 0)
        pos = t * rows + b * BLOCK + lax.rem(row, BLOCK)
        start = doc_start(pos)
        key_pos = (t - back) * rows + b * BLOCK + lax.broadcasted_iota(jnp.int32, (1, reach), 1)
        allowed = (key_pos >= start) & (key_pos <= pos)
        scores = jnp.where(allowed, scores, masked_score)
        peak = jnp.max(scores, axis=-1, keepdims=True)
        weights = jnp.exp(scores - peak)
        denom = jnp.sum(weights, axis=-1, keepdims=True)
        mixed = jnp.dot(weights.astype(jnp.bfloat16), values, preferred_element_type=jnp.float32)
        mixed = (mixed / denom).astype(jnp.bfloat16)
        spread = peak + jnp.log(denom)
        for h in range(heads_here):
            att[mine, b, :, h * HEAD : (h + 1) * HEAD] = mixed[h * BLOCK : (h + 1) * BLOCK]
            lse_mine[pl.ds(b * heads_here + h, 1), :] = jnp.sum(
                jnp.where(diagonal, spread[h * BLOCK : (h + 1) * BLOCK], 0.0),
                axis=0,
                keepdims=True,
            )
        for dx in range(1, heads):
            send(
                True,
                att.at[mine, b],
                att.at[mine, b],
                a_send.at[dx, b],
                a_recv.at[x, b],
                (y, t, lax.rem(x + dx, heads), c),
            )
        send(
            True,
            att.at[mine, b],
            att.at[mine, b],
            ac_send.at[0, b],
            ac_recv.at[x, b],
            (y, t, x, twin),
        )
        if b:
            forward(b - 1)

    me = t * subs + c
    for dt in range(toks):
        for dc in range(subs):
            if dt or dc:
                send(
                    True,
                    lse_mine,
                    lse_all.at[me],
                    l_send.at[dt * subs + dc],
                    l_recv.at[me],
                    (y, lax.rem(t + dt, toks), x, lax.rem(c + dc, subs)),
                )
    lse_all[me] = lse_mine[...]

    for r in range(shares):
        for side in range(2):
            dst = wo.at[r, pl.ds(side * o_half, o_half)]
            arrived(True, dst, o_recv.at[r, side])
    share_cols = out_ref.shape[1]
    columns = pl.ds(pl.multiple_of(mine * share_cols, share_cols), share_cols)
    pair = 2
    for first in range(0, blocks, pair):
        if first + pair == blocks:
            forward(blocks - 1)
        for b in range(first, first + pair):
            for dx in range(heads):
                source = lax.rem(x + dx, heads)
                arrived(True, att.at[source * subs + twin, b], ac_recv.at[source, b])
        at = slice(first * BLOCK, (first + pair) * BLOCK)
        summed = jnp.zeros((pair * BLOCK, share_cols), jnp.float32)
        for r in range(shares):
            product = jnp.dot(
                att[r, first : first + pair].reshape(pair * BLOCK, att.shape[3]),
                wo[r],
                preferred_element_type=jnp.float32,
            )
            summed += product.astype(jnp.bfloat16).astype(jnp.float32)
        out_ref[at, :] = (hid[at, columns].astype(jnp.float32) + summed).astype(jnp.bfloat16)

    group_heads = heads_here * subs
    for dt in range(toks):
        for dc in range(subs):
            source = lax.rem(t + dt, toks) * subs + lax.rem(c + dc, subs)
            if dt or dc:
                arrived(True, lse_all.at[source], l_recv.at[source])
    for source in range(toks * subs):
        kept = jnp.zeros((1, BLOCK), jnp.float32)
        for task in range(tasks):
            server = table_ref[
                (source // subs) * blocks + task // heads_here,
                x * group_heads + (source % subs) * heads_here + task % heads_here,
            ]
            kept = kept + jnp.where(server == me, lse_all[source, task : task + 1, :], 0.0)
        lse_ref[source : source + 1, :] = kept

    for cond, copy in sent:
        when(cond, copy.wait_send)


def body(sizes, hidden_in, norm_gain, q_weight, kv_weight, o_weight, doc_lengths, task_server):
    groups, toks, heads, subs = sizes
    rows, width = hidden_in.shape
    depth, q_cols = q_weight.shape
    o_rows, o_cols = o_weight.shape
    shares = heads * subs
    assert groups == 2 and subs == 2 and toks == shares
    assert width // shares == o_cols and DOCMAX % rows == 0
    blocks = rows // BLOCK
    heads_here = q_cols // HEAD
    back = DOCMAX // rows
    tasks = blocks * heads_here
    servers = toks * subs
    half = jnp.arange(HEAD // 2, dtype=jnp.float32)
    freq = rope_base ** (-(half * 2.0 / HEAD))
    freq = jnp.concatenate([freq, freq])[None, :]
    bf16, f32 = jnp.bfloat16, jnp.float32
    dma = pltpu.SemaphoreType.DMA
    any_spec = pl.BlockSpec(memory_space=pl.ANY)
    vmem = pl.BlockSpec(memory_space=pltpu.VMEM)
    smem = pl.BlockSpec(memory_space=pltpu.SMEM)
    layer_out, lse = pl.pallas_call(
        functools.partial(kernel, sizes),
        out_shape=(
            jax.ShapeDtypeStruct((rows, o_cols), bf16),
            jax.ShapeDtypeStruct((servers, BLOCK), f32),
        ),
        in_specs=[smem, smem, any_spec, vmem, vmem, any_spec, any_spec, any_spec],
        out_specs=(vmem, vmem),
        scratch_shapes=[
            pltpu.VMEM((rows, width), bf16),
            pltpu.VMEM((toks, 2, rows, depth // 2), bf16),
            pltpu.VMEM((toks, depth, q_cols), bf16),
            pltpu.VMEM((toks, depth, HEAD), bf16),
            pltpu.VMEM((toks, o_rows // 2, o_cols), bf16),
            pltpu.VMEM((shares, o_rows, o_cols), bf16),
            pltpu.VMEM((rows, q_cols), f32),
            pltpu.VMEM((rows, HEAD), f32),
            pltpu.VMEM((rows, HEAD), f32),
            pltpu.VMEM((rows, HEAD), f32),
            pltpu.VMEM((blocks, heads_here * BLOCK, HEAD), bf16),
            pltpu.VMEM((2, (back + 1) * rows, HEAD), bf16),
            pltpu.VMEM((shares, blocks, BLOCK, q_cols), bf16),
            pltpu.VMEM((tasks, BLOCK), f32),
            pltpu.VMEM((servers, tasks, BLOCK), f32),
            dma((3,)),
            dma((3, 2, toks)),
            dma((3, toks)),
            dma((2, toks)),
            dma((2, toks)),
            dma((toks, groups)),
            dma((shares, 2)),
            dma((back,)),
            dma((back,)),
            dma((back + 1,)),
            dma((back + 1,)),
            dma((heads, blocks)),
            dma((heads, blocks)),
            dma((heads, blocks)),
            dma((heads, blocks)),
            dma((servers,)),
            dma((servers,)),
        ],
        compiler_params=pltpu.CompilerParams(
            collective_id=0, has_side_effects=True, vmem_limit_bytes=56 * 1024 * 1024
        ),
        cost_estimate=pl.CostEstimate(
            flops=4 * 10**9, bytes_accessed=8 * 2**20, transcendentals=2 * 10**6
        ),
    )(
        doc_lengths,
        task_server,
        hidden_in,
        norm_gain[None, :],
        freq,
        q_weight,
        kv_weight,
        o_weight,
    )
    return (layer_out, lse.reshape(1, servers, 1, BLOCK))


def solution(mesh):
    placed = (
        P(("group", "tok"), None),
        P(),
        P("tok", ("head", "sub")),
        P("tok", ("head", "sub")),
        P(("head", "sub"), "tok"),
        P("group"),
        P("group", None),
    )
    sizes = tuple(mesh.shape[name] for name in ("group", "tok", "head", "sub"))
    return jax.shard_map(
        functools.partial(body, sizes),
        mesh=mesh,
        in_specs=placed,
        out_specs=(
            P(("group", "tok"), ("head", "sub")),
            P(("group", "tok", "sub"), None, "head", None),
        ),
        check_vma=False,
    )
```
